32 devices in a mesh: ctx: 8 (over z, x), tp: 4 (over y, core).
Axes of the slice: x: 2, y: 2, z: 4, core: 2. Of those that a mesh axis runs over, the one named last changes fastest.
Arguments:
- query_in: bfloat16 [2048, 1024], P('tp', 'ctx'), may hold values from -6 to 6
- key_in: bfloat16 [2048, 1024], P('tp', 'ctx'), may hold values from -6 to 6
- value_in: bfloat16 [2048, 1024], P('tp', 'ctx'), may hold values from -6 to 6
- short_weights: float32 [3, 2048, 7], P(None, 'tp'), may hold values from -3 to 3
- filters: float32 [4, 512, 1024], P('tp', 'ctx'), may hold values from 0 to 1
- out_weight: bfloat16 [4096, 2048], P(None, 'tp'), may hold values from -0.125 to 0.125
- cotangent: bfloat16 [4096, 1024], P('tp', 'ctx'), may hold values from -6 to 6
Outputs:
- mixed_out: bfloat16 [4096, 1024], P('tp', 'ctx')
- grad_query: bfloat16 [2048, 1024], P('tp', 'ctx')
- grad_key: bfloat16 [2048, 1024], P('tp', 'ctx')
- grad_value: bfloat16 [2048, 1024], P('tp', 'ctx')
- grad_filters: float32 [4, 512, 1024], P('tp', 'ctx')
- grad_out_weight: float32 [4096, 2048], P('ctx', 'tp')
The draws below stay inside these ranges and needn't reach their ends.
All inputs are finite; a program needn't handle non-finite values.
Results may differ from the reference program's by a relative error of at most 0.012.
Values may be sent and summed in bfloat16 or wider, within the bound.
A program may use at most 128 MiB of HBM per device.

```python
import math
import jax
import jax.numpy as jnp

D = 4096
C = 2048
TAPS = 7
CONTEXT_SPAN = 1024
TPG = 4
CT = 512


def draw_filters(key, part):
    lookup_fragments = jax.random.split(jax.random.fold_in(key, 11), 5)
    shape = (TPG, CT, CONTEXT_SPAN)
    element_indices = jnp.arange(CONTEXT_SPAN, dtype=jnp.float32)
    chooser = jax.random.uniform(lookup_fragments[0], (TPG, CT, 1), jnp.float32)
    slow_mask = chooser < 0.5
    rough = jax.random.uniform(lookup_fragments[4], shape, jnp.float32, 0.4, 1.6)
    slow_rate = jnp.exp(jax.random.uniform(lookup_fragments[1], (TPG, CT, 1), jnp.float32, math.log(0.3 / CONTEXT_SPAN), math.log(2.0 / CONTEXT_SPAN)))
    fast_rate = jnp.exp(jax.random.uniform(lookup_fragments[2], (TPG, CT, 1), jnp.float32, math.log(1.0 / 60.0), math.log(1.0 / 20.0)))
    rate = jnp.where(slow_mask, slow_rate, fast_rate)
    cluster_batches = jax.random.randint(lookup_fragments[3], (3,), 1, CONTEXT_SPAN).astype(jnp.float32)
    discarded_entries = jnp.ones((CONTEXT_SPAN,), jnp.float32)
    for chosen_portion in range(3):
        discarded_entries = discarded_entries * jnp.where(element_indices >= cluster_batches[chosen_portion], 0.6, 1.0)
    amplitude = jnp.sqrt(2.0 * rate)
    return amplitude * jnp.exp(-rate * element_indices) * discarded_entries * rough


def spiked(values, own_key, source, target, shards_of, factor):
    owner, partner = [(jnp.arange(values.shape[axis_at]) // (values.shape[axis_at] // shards_of)).reshape([-1 if axis == axis_at else 1 for axis in range(values.ndim)]) for axis_at in (source, target)]
    chosen = jax.random.permutation(own_key, shards_of)[partner]
    strong = (owner == chosen) | (owner == (partner + shards_of // 2) % shards_of)
    return jnp.where(strong, factor * values, values)


def level_of(rng, shape, shards, smallest, top_value):
    gain = 1.0
    for position, parts in shards:
        heights = jax.random.uniform(jax.random.fold_in(jax.random.fold_in(rng, 6), position), (parts,), jnp.float32, smallest / len(shards), top_value / len(shards))
        gain = gain * jnp.repeat(jnp.exp(heights), shape[position] // parts).reshape((-1,) + (1,) * (len(shape) - 1 - position))
    return gain


def scatter_about(own_key, dims, spread, most, cuts=(), held_as=jnp.bfloat16):
    gain = level_of(own_key, dims, cuts, -0.22, 0.18) if cuts else 1.0
    values = jax.random.normal(own_key, dims, jnp.float32) * spread * gain
    return jnp.minimum(jnp.maximum(values, -most), most).astype(held_as)


def heavy_noise(key, extent, deviation, reach, cuts, heavy, kind=jnp.bfloat16):
    array = deviation * jax.random.normal(key, extent, jnp.float32)
    if cuts:
        array = array * level_of(key, extent, cuts, -0.22, 0.18)
    return jnp.clip(spiked(array, jax.random.fold_in(key, 3), *heavy), -reach, reach).astype(kind)


def setup_inputs(seed: int = 0) -> dict:
    streams_of = jax.random.split(jax.random.key(seed), 8)
    query_in = scatter_about(streams_of[0], (C, CONTEXT_SPAN), 1.0, 6.0, ((0, 4), (1, 8)))
    key_in = scatter_about(streams_of[1], (C, CONTEXT_SPAN), 1.0, 6.0, ((0, 4), (1, 8)))
    value_in = scatter_about(streams_of[2], (C, CONTEXT_SPAN), 1.0, 6.0, ((0, 4), (1, 8)))
    short_weights = scatter_about(streams_of[3], (3, C, TAPS), 0.4, 3.0, ((1, 4),), jnp.float32)
    filters = draw_filters(jax.random.fold_in(streams_of[7], 71), 0)
    out_weight = scatter_about(streams_of[5], (D, C), C ** -0.5, 0.125, ((1, 4),))
    cotangent = heavy_noise(streams_of[6], (D, CONTEXT_SPAN), 1.0, 6.0, ((0, 4), (1, 8)), (1, 0, 8, 2.0))
    return {"query_in": query_in, "key_in": key_in, "value_in": value_in, "short_weights": short_weights, "filters": filters, "out_weight": out_weight, "cotangent": cotangent}


def causal_taps(stacked, weights):
    tap_count = weights.shape[2]
    length = stacked.shape[2]
    padded = jnp.pad(stacked.astype(jnp.float32), ((0, 0), (0, 0), (tap_count - 1, 0)))
    running_total = jnp.zeros(stacked.shape, jnp.float32)
    for offset in range(tap_count):
        begin = tap_count - 1 - offset
        running_total = running_total + weights[:, :, offset:offset + 1] * padded[:, :, begin:begin + length]
    return running_total


def anticausal_taps(stacked, weights):
    tap_count = weights.shape[2]
    length = stacked.shape[2]
    padded = jnp.pad(stacked.astype(jnp.float32), ((0, 0), (0, 0), (0, tap_count - 1)))
    running_total = jnp.zeros(stacked.shape, jnp.float32)
    for offset in range(tap_count):
        running_total = running_total + weights[:, :, offset:offset + 1] * padded[:, :, offset:offset + length]
    return running_total


def reference(query_in, key_in, value_in, short_weights, filters, out_weight, cotangent):
    full_len = 2 * CONTEXT_SPAN
    shorts = causal_taps(jnp.stack([query_in, key_in, value_in]), short_weights).astype(jnp.bfloat16)
    product = (shorts[1].astype(jnp.float32) * shorts[2].astype(jnp.float32)).astype(jnp.bfloat16)
    kernel = filters.reshape(C, CONTEXT_SPAN)
    kernel_spec = jnp.fft.rfft(kernel, n=full_len, axis=1)
    product_spec = jnp.fft.rfft(product.astype(jnp.float32), n=full_len, axis=1)
    convolved = jnp.fft.irfft(product_spec * kernel_spec, n=full_len, axis=1)[:, :CONTEXT_SPAN].astype(jnp.bfloat16)
    gated_out = (shorts[0].astype(jnp.float32) * convolved.astype(jnp.float32)).astype(jnp.bfloat16)
    mixed_out = jnp.dot(out_weight, gated_out, preferred_element_type=jnp.float32).astype(jnp.bfloat16)
    grad_gated = jnp.dot(out_weight.T, cotangent, preferred_element_type=jnp.float32)
    grad_out_weight = jnp.dot(cotangent, gated_out.T, preferred_element_type=jnp.float32)
    grad_conv = (grad_gated * shorts[0].astype(jnp.float32)).astype(jnp.bfloat16)
    grad_spec = jnp.fft.rfft(grad_conv.astype(jnp.float32), n=full_len, axis=1)
    derivative_of_multiple = jnp.fft.irfft(jnp.conj(kernel_spec) * grad_spec, n=full_len, axis=1)[:, :CONTEXT_SPAN].astype(jnp.bfloat16)
    grad_filters = jnp.fft.irfft(jnp.conj(product_spec) * grad_spec, n=full_len, axis=1)[:, :CONTEXT_SPAN].reshape(filters.shape)
    grad_shorts = jnp.stack([
        grad_gated * convolved.astype(jnp.float32),
        derivative_of_multiple.astype(jnp.float32) * shorts[2].astype(jnp.float32),
        derivative_of_multiple.astype(jnp.float32) * shorts[1].astype(jnp.float32)]).astype(jnp.bfloat16)
    gradients = anticausal_taps(grad_shorts, short_weights).astype(jnp.bfloat16)
    return mixed_out, gradients[0], gradients[1], gradients[2], grad_filters, grad_out_weight
```

```python
import functools

import jax
import jax.numpy as jnp
import numpy as np
from jax import lax
from jax.experimental import pallas as pl
from jax.experimental.pallas import tpu as pltpu
from jax.sharding import PartitionSpec as P

F32 = jnp.float32
BF16 = jnp.bfloat16
MESH = pl.DeviceIdType.MESH


def split_table(table):
    table = table.astype(np.float32)
    high = table.astype(jnp.bfloat16)
    low = (table - high.astype(np.float32)).astype(jnp.bfloat16)
    return high, low


def make_tables(blocks, width):
    rows = 2 * blocks
    full = rows * width
    kept = blocks + 1
    turn = np.outer(np.arange(kept), np.arange(blocks)) % rows * (2 * np.pi / rows)
    outer = np.stack([np.cos(turn), -np.sin(turn)]).astype(np.float32)
    twist = np.outer(np.arange(kept), np.arange(width)) % full * (2 * np.pi / full)
    weight = np.full((kept, 1), 2.0 / full)
    weight[0] = weight[-1] = 1.0 / full
    twists = np.stack(
        [np.cos(twist), -np.sin(twist), weight * np.cos(twist), weight * -np.sin(twist)]
    ).astype(np.float32)[:, :, None, :]
    inner = np.outer(np.arange(width), np.arange(width)) % width * (2 * np.pi / width)
    re, im = np.cos(inner), -np.sin(inner)
    forward = np.block([[re, im], [-im, re]])
    backward = np.block([[re, -im], [im, re]])
    return outer, twists, *split_table(forward), *split_table(backward)


def dot(a, b):
    return jnp.dot(a, b, preferred_element_type=F32)


def dot_split(value, high, low):
    value_high = value.astype(BF16)
    value_low = (value - value_high.astype(F32)).astype(BF16)
    return dot(value_high, high) + dot(value_low, high) + dot(value_high, low)


def merge_rows(value):
    blocks, rows, lanes = value.shape
    if rows % 16:
        return value.astype(F32).reshape(blocks * rows, lanes).astype(BF16)
    return value.reshape(blocks * rows, lanes)


def kernel(
    nctx,
    ntp,
    outer,
    query,
    key,
    value,
    taps,
    filters,
    weight_hbm,
    cot,
    twists,
    fwd_high,
    fwd_low,
    bwd_high,
    bwd_low,
    mixed_out,
    grad_query,
    grad_key,
    grad_value,
    grad_filters,
    grad_weight,
    weight,
    full_cot,
    cot_rows,
    inputs,
    shorts,
    signal,
    work,
    parts,
    spec_f,
    spec_p,
    spec_g,
    convolved,
    gated,
    gated_here,
    gated_all,
    gate_out,
    gate_chan,
    shorts_grad,
    grads,
    partial,
    pair_in,
    pair_sum,
    final_in,
    local_sem,
    in_s,
    in_r,
    cot_s,
    cot_r,
    rows_s,
    rows_r,
    quart_s,
    quart_r,
    gate_s,
    gate_r,
    here_s,
    here_r,
    all_s,
    all_r,
    fwd_s,
    fwd_r,
    back_s,
    back_r,
    pair_s,
    pair_r,
    final_s,
    final_r,
):
    channels, width = query.shape[1:]
    kept = nctx + 1
    tap_count = taps.shape[3]
    me = lax.axis_index("ctx")
    mine = lax.axis_index("tp")
    core_mate = mine + 1 - 2 * (mine % 2)
    side_mate = (mine + ntp // 2) % ntp
    far_mate = (core_mate + ntp // 2) % ntp
    x_mate = me + 1 - 2 * (me % 2)
    share = nctx // ntp

    def send(src, dst, send_sem, recv_sem, device):
        copy = pltpu.make_async_remote_copy(
            src_ref=src,
            dst_ref=dst,
            send_sem=send_sem,
            recv_sem=recv_sem,
            device_id=device,
            device_id_type=MESH,
        )
        copy.start()
        return copy

    def peer(step):
        return lax.rem(me + step, nctx)

    def at_ctx(target):
        return (target, mine)

    def at_tp(target):
        return (me, target)

    load_weight = pltpu.make_async_copy(weight_hbm, weight, local_sem)
    load_weight.start()

    barrier = pltpu.get_barrier_semaphore()
    for step in range(1, nctx):
        pl.semaphore_signal(barrier, inc=1, device_id=at_ctx(peer(step)), device_id_type=MESH)
    for mate in (core_mate, side_mate):
        pl.semaphore_signal(barrier, inc=1, device_id=at_tp(mate), device_id_type=MESH)
    pl.semaphore_wait(barrier, nctx + 1)

    sent = []

    own_rows = full_cot.at[pl.ds(mine * share, share)]
    to_side = send(cot, own_rows, cot_s.at[0], cot_r.at[0], at_tp(side_mate))
    to_core = send(cot, own_rows, cot_s.at[1], cot_r.at[1], at_tp(core_mate))
    sent += [to_side, to_core]
    in_copies = []
    for step in range(1, nctx):
        target = peer(step)
        for index, source in enumerate((query, key, value)):
            copy = send(
                source.at[target],
                inputs.at[index, me + 1],
                in_s.at[index, step],
                in_r.at[index, step],
                at_ctx(target),
            )
            in_copies.append(copy)
    sent += in_copies
    for index, source in enumerate((query, key, value)):
        inputs[index, me + 1] = source[me]
        inputs[index, 0] = jnp.zeros((channels, width), BF16)
        shorts_grad[index, nctx] = jnp.zeros((channels, width), BF16)
    full_cot[pl.ds(mine * share, share)] = cot[...]

    def spectrum(spec):
        def one(k, carry):
            re = jnp.zeros((channels, width), F32)
            im = jnp.zeros((channels, width), F32)
            for n in range(nctx):
                block = signal[n]
                re = re + outer[0, k, n] * block
                im = im + outer[1, k, n] * block
            cos, sin = twists[0, k], twists[1, k]
            rows = pl.ds(pl.multiple_of(k * channels, channels), channels)
            work[rows, :width] = re * cos - im * sin
            work[rows, width:] = re * sin + im * cos
            return carry

        lax.fori_loop(0, kept, one, 0)
        spec[...] = dot_split(work[...], fwd_high[...], fwd_low[...])

    def inverse(re, im, store):
        work[:, :width] = re
        work[:, width:] = im
        work[...] = dot_split(work[...], bwd_high[...], bwd_low[...])

        def turn(k, carry):
            rows = pl.ds(pl.multiple_of(k * channels, channels), channels)
            back_re, back_im = work[rows, :width], work[rows, width:]
            cos, sin = twists[2, k], twists[3, k]
            parts[0, k] = back_re * cos + back_im * sin
            parts[1, k] = back_im * cos - back_re * sin
            return carry

        lax.fori_loop(0, kept, turn, 0)

        def one(n, carry):
            total = parts[0, 0]
            for k in range(1, kept):
                total = total + outer[0, k, n] * parts[0, k]
                if k < nctx:
                    total = total + outer[1, k, n] * parts[1, k]
            store(n, total)
            return carry

        lax.fori_loop(0, nctx, one, 0)

    lane = lax.broadcasted_iota(jnp.int32, (channels, width), 1)

    for n in range(nctx):
        signal[n] = filters[:, n * width : (n + 1) * width]
    spectrum(spec_f)

    to_side.wait_recv()
    passed_rows = full_cot.at[pl.ds(side_mate * share, share)]
    passed = send(passed_rows, passed_rows, cot_s.at[2], cot_r.at[2], at_tp(core_mate))
    sent.append(passed)
    to_core.wait_recv()
    load_weight.wait()
    passed.wait_recv()

    block_rows = cot.shape[0] * cot.shape[1] * cot.shape[2]
    total = jnp.zeros((width, nctx * channels), F32)
    for group in range(ntp):
        cot_block = full_cot[group * share : (group + 1) * share].reshape(block_rows, width)
        total = total + lax.dot_general(
            cot_block,
            weight[group * block_rows : (group + 1) * block_rows, :],
            (((0,), (0,)), ((), ())),
            preferred_element_type=F32,
        )
    gate_out[...] = total.T.reshape(nctx, channels, width).astype(BF16)
    gate_copies = []
    for step in range(1, nctx):
        target = peer(step)
        gate_copies.append(
            send(
                gate_out.at[target],
                gate_chan.at[me],
                gate_s.at[step],
                gate_r.at[step],
                at_ctx(target),
            )
        )
    sent += gate_copies
    gate_chan[me] = gate_out[me]

    for copy in in_copies:
        copy.wait_recv()

    row_copies = []
    for step in range(1, nctx):
        target = peer(step)
        row_copies.append(
            send(
                full_cot.at[target, mine],
                cot_rows.at[mine, me],
                rows_s.at[step],
                rows_r.at[step],
                at_ctx(target),
            )
        )
    sent += row_copies
    cot_rows[mine, me] = full_cot[me, mine]

    for index in range(3):
        tap = taps[index, me]

        def short(n, carry, index=index, tap=tap):
            before = inputs[index, n].astype(F32)
            here = inputs[index, n + 1].astype(F32)
            total = tap[:, 0:1] * here
            for j in range(1, tap_count):
                moved = jnp.where(lane < j, pltpu.roll(before, j, 1), pltpu.roll(here, j, 1))
                total = total + tap[:, j : j + 1] * moved
            shorts[index, n] = total.astype(BF16)
            return carry

        lax.fori_loop(0, nctx, short, 0)

    def multiply(n, carry):
        product = shorts[1, n].astype(F32) * shorts[2, n].astype(F32)
        signal[n] = product.astype(BF16).astype(F32)
        return carry

    lax.fori_loop(0, nctx, multiply, 0)
    spectrum(spec_p)

    f_re, f_im = spec_f[:, :width], spec_f[:, width:]
    p_re, p_im = spec_p[:, :width], spec_p[:, width:]

    def store_convolved(n, total):
        rounded = total.astype(BF16)
        convolved[n] = rounded
        gated[n] = (shorts[0, n].astype(F32) * rounded.astype(F32)).astype(BF16)

    inverse(p_re * f_re - p_im * f_im, p_re * f_im + p_im * f_re, store_convolved)

    here_copies = []
    for step in range(1, nctx):
        target = peer(step)
        here_copies.append(
            send(
                gated.at[target],
                gated_here.at[me],
                here_s.at[step],
                here_r.at[step],
                at_ctx(target),
            )
        )
    sent += here_copies
    to_x = send(gated, gated_all.at[me], fwd_s.at[0], fwd_r.at[0], at_ctx(x_mate))
    all_copies = [
        send(gated, gated_all.at[me], all_s.at[step], all_r.at[step], at_ctx(peer(step)))
        for step in range(2, nctx, 2)
    ]
    sent += [to_x] + all_copies
    gated_here[me] = gated[me]
    gated_all[me] = gated[...]

    for copy in row_copies:
        copy.wait_recv()
    own_quarter = cot_rows.at[mine]
    quarter_side = send(own_quarter, own_quarter, quart_s.at[0], quart_r.at[0], at_tp(side_mate))
    quarter_core = send(own_quarter, own_quarter, quart_s.at[1], quart_r.at[1], at_tp(core_mate))
    sent += [quarter_side, quarter_core]

    for copy in gate_copies:
        copy.wait_recv()

    def to_conv(n, carry):
        grad_conv = gate_chan[n].astype(F32) * shorts[0, n].astype(F32)
        signal[n] = grad_conv.astype(BF16).astype(F32)
        return carry

    lax.fori_loop(0, nctx, to_conv, 0)
    spectrum(spec_g)

    for copy in here_copies:
        copy.wait_recv()
    right = merge_rows(gated_here[...])

    def project(group):
        start = pl.multiple_of(group * block_rows, block_rows)
        return dot(weight[pl.ds(start, block_rows), :], right)

    core = mine % 2
    pair_copies = []
    for side in range(ntp // 2):
        partial[side] = project(2 * side + 1 - core).astype(BF16)
        pair_copies.append(
            send(
                partial.at[side],
                pair_in.at[side],
                pair_s.at[side],
                pair_r.at[side],
                at_tp(core_mate),
            )
        )
    sent += pair_copies

    f_re, f_im = spec_f[:, :width], spec_f[:, width:]
    g_re, g_im = spec_g[:, :width], spec_g[:, width:]

    def store_product(n, total):
        rounded = total.astype(BF16).astype(F32)
        gate = gate_chan[n].astype(F32)
        shorts_grad[0, n] = (gate * convolved[n].astype(F32)).astype(BF16)
        shorts_grad[1, n] = (rounded * shorts[2, n].astype(F32)).astype(BF16)
        shorts_grad[2, n] = (rounded * shorts[1, n].astype(F32)).astype(BF16)

    inverse(f_re * g_re + f_im * g_im, f_re * g_im - f_im * g_re, store_product)

    for index in range(3):
        tap = taps[index, me]

        def long(n, carry, index=index, tap=tap):
            here = shorts_grad[index, n].astype(F32)
            after = shorts_grad[index, n + 1].astype(F32)
            total = tap[:, 0:1] * here
            for j in range(1, tap_count):
                moved = jnp.where(
                    lane < width - j,
                    pltpu.roll(here, width - j, 1),
                    pltpu.roll(after, width - j, 1),
                )
                total = total + tap[:, j : j + 1] * moved
            grads[index, n] = total.astype(BF16)
            return carry

        lax.fori_loop(0, nctx, long, 0)
    results = (grad_query, grad_key, grad_value)
    back_copies = []
    for step in range(1, nctx):
        target = peer(step)
        for index, result in enumerate(results):
            back_copies.append(
                send(
                    grads.at[index, target],
                    result.at[me],
                    back_s.at[index, step],
                    back_r.at[index, step],
                    at_ctx(target),
                )
            )
    sent += back_copies
    for index, result in enumerate(results):
        result[me] = grads[index, me]

    my_side = mine // 2
    for copy in pair_copies:
        copy.wait_recv()
    other = 1 - my_side
    pair_sum[...] = (project(side_mate) + pair_in[other].astype(F32)).astype(BF16)
    final = send(pair_sum, final_in, final_s, final_r, at_tp(side_mate))
    sent.append(final)

    passed_all = []
    for copy, step in zip(all_copies, range(2, nctx, 2)):
        copy.wait_recv()
        block = gated_all.at[lax.rem(me + nctx - step, nctx)]
        passed_all.append(
            send(block, block, fwd_s.at[step // 2], fwd_r.at[step // 2], at_ctx(x_mate))
        )
    sent += passed_all
    quarter_side.wait_recv()
    far_quarter = cot_rows.at[side_mate]
    quarter_far = send(far_quarter, far_quarter, quart_s.at[2], quart_r.at[2], at_tp(core_mate))
    sent.append(quarter_far)

    own_sum = project(mine) + pair_in[my_side].astype(F32)

    p_re, p_im = spec_p[:, :width], spec_p[:, width:]
    g_re, g_im = spec_g[:, :width], spec_g[:, width:]

    def store_filters(n, total):
        grad_filters[:, pl.ds(pl.multiple_of(n * width, width), width)] = total

    inverse(p_re * g_re + p_im * g_im, p_re * g_im - p_im * g_re, store_filters)

    final.wait_recv()
    mixed_out[...] = (own_sum + final_in[...].astype(F32)).astype(BF16)

    quarter_core.wait_recv()
    quarter_far.wait_recv()
    to_x.wait_recv()
    for copy in passed_all:
        copy.wait_recv()
    quarter = cot_rows.shape[2]

    def weigh(n, totals):
        right = merge_rows(gated_all[:, n])
        left = cot_rows[:, n].reshape(ntp * quarter, width)
        grad_weight[...] += lax.dot_general(
            left, right, (((1,), (1,)), ((), ())), preferred_element_type=F32
        )
        return totals

    grad_weight[...] = jnp.zeros_like(grad_weight)
    lax.fori_loop(0, nctx, weigh, 0)

    for copy in back_copies:
        copy.wait_recv()
    for copy in sent:
        copy.wait_send()


def per_device(nctx, ntp, query_in, key_in, value_in, short_weights, filters, out_weight, cotangent):
    rows, width = query_in.shape
    channels = rows // nctx
    features = out_weight.shape[0]
    quarter = features // (nctx * ntp)
    share = nctx // ntp
    kept = nctx + 1
    outer, twists, *inner = make_tables(nctx, width)
    tap_count = short_weights.shape[2]
    blocks = (nctx, channels, width)

    def bf(*shape):
        return pltpu.VMEM(shape, BF16)

    def f32(*shape):
        return pltpu.VMEM(shape, F32)

    def sems(*shape):
        return pltpu.SemaphoreType.DMA(shape)

    vmem = pl.BlockSpec(memory_space=pltpu.VMEM)
    smem = pl.BlockSpec(memory_space=pltpu.SMEM)
    outs = pl.pallas_call(
        functools.partial(kernel, nctx, ntp),
        out_shape=(
            jax.ShapeDtypeStruct((features // ntp, width), BF16),
            jax.ShapeDtypeStruct(blocks, BF16),
            jax.ShapeDtypeStruct(blocks, BF16),
            jax.ShapeDtypeStruct(blocks, BF16),
            jax.ShapeDtypeStruct((channels, nctx * width), F32),
            jax.ShapeDtypeStruct((features // nctx, rows), F32),
        ),
        in_specs=[smem] + [vmem] * 5 + [pl.BlockSpec(memory_space=pl.ANY)] + [vmem] * 6,
        out_specs=tuple([vmem] * 6),
        scratch_shapes=[
            bf(features, rows),
            bf(nctx, ntp, quarter, width),
            bf(ntp, nctx, quarter, width),
            bf(3, nctx + 1, channels, width),
            bf(3, *blocks),
            f32(*blocks),
            f32(kept * channels, 2 * width),
            f32(2, kept, channels, width),
            f32(kept * channels, 2 * width),
            f32(kept * channels, 2 * width),
            f32(kept * channels, 2 * width),
            bf(*blocks),
            bf(*blocks),
            bf(*blocks),
            bf(nctx, *blocks),
            bf(*blocks),
            bf(*blocks),
            bf(3, nctx + 1, channels, width),
            bf(3, *blocks),
            bf(ntp // 2, features // ntp, width),
            bf(ntp // 2, features // ntp, width),
            bf(features // ntp, width),
            bf(features // ntp, width),
            pltpu.SemaphoreType.DMA,
            sems(3, nctx),
            sems(3, nctx),
            sems(3),
            sems(3),
            sems(nctx),
            sems(nctx),
            sems(3),
            sems(3),
            sems(nctx),
            sems(nctx),
            sems(nctx),
            sems(nctx),
            sems(nctx),
            sems(nctx),
            sems(nctx),
            sems(nctx),
            sems(3, nctx),
            sems(3, nctx),
            sems(ntp // 2),
            sems(ntp // 2),
            pltpu.SemaphoreType.DMA,
            pltpu.SemaphoreType.DMA,
        ],
        compiler_params=pltpu.CompilerParams(
            collective_id=0, has_side_effects=True, vmem_limit_bytes=56 * 1024 * 1024
        ),
        cost_estimate=pl.CostEstimate(
            flops=6 * features * rows * width, bytes_accessed=10 * features * rows // 4, transcendentals=0
        ),
        name="mixer",
    )(
        jnp.asarray(outer),
        query_in.reshape(blocks),
        key_in.reshape(blocks),
        value_in.reshape(blocks),
        short_weights.reshape(3, nctx, channels, tap_count),
        filters.reshape(channels, nctx * width),
        out_weight,
        cotangent.reshape(share, ntp, quarter, width),
        jnp.asarray(twists),
        *[jnp.asarray(table) for table in inner],
    )
    mixed, grad_query, grad_key, grad_value, grad_filters, grad_weight = outs
    return (
        mixed,
        grad_query.reshape(rows, width),
        grad_key.reshape(rows, width),
        grad_value.reshape(rows, width),
        grad_filters.reshape(filters.shape),
        grad_weight,
    )


def solution(mesh):
    placed = (
        P("tp", "ctx"),
        P("tp", "ctx"),
        P("tp", "ctx"),
        P(None, "tp", None),
        P("tp", "ctx", None),
        P(None, "tp"),
        P("tp", "ctx"),
    )
    return jax.shard_map(
        functools.partial(per_device, mesh.shape["ctx"], mesh.shape["tp"]),
        mesh=mesh,
        in_specs=placed,
        out_specs=(
            P("tp", "ctx"),
            P("tp", "ctx"),
            P("tp", "ctx"),
            P("tp", "ctx"),
            P("tp", "ctx", None),
            P("ctx", "tp"),
        ),
        check_vma=False,
    )
```

```python
import functools

import jax
import jax.numpy as jnp
import numpy as np
from jax import lax
from jax.experimental import pallas as pl
from jax.experimental.pallas import tpu as pltpu
from jax.sharding import PartitionSpec as P

F32 = jnp.float32
BF16 = jnp.bfloat16
MESH = pl.DeviceIdType.MESH


def split_table(table):
    table = table.astype(np.float32)
    high = table.astype(jnp.bfloat16)
    low = (table - high.astype(np.float32)).astype(jnp.bfloat16)
    return high, low


def make_tables(blocks, width):
    rows = 2 * blocks
    full = rows * width
    kept = blocks + 1
    turn = np.outer(np.arange(kept), np.arange(blocks)) % rows * (2 * np.pi / rows)
    outer = np.stack([np.cos(turn), -np.sin(turn)]).astype(np.float32)
    twist = np.outer(np.arange(kept), np.arange(width)) % full * (2 * np.pi / full)
    weight = np.full((kept, 1), 2.0 / full)
    weight[0] = weight[-1] = 1.0 / full
    twists = np.stack(
        [np.cos(twist), -np.sin(twist), weight * np.cos(twist), weight * -np.sin(twist)]
    ).astype(np.float32)[:, :, None, :]
    inner = np.outer(np.arange(width), np.arange(width)) % width * (2 * np.pi / width)
    re, im = np.cos(inner), -np.sin(inner)
    forward = np.block([[re, im], [-im, re]])
    backward = np.block([[re, -im], [im, re]])
    return outer, twists, *split_table(forward), *split_table(backward)


def dot(a, b):
    return jnp.dot(a, b, preferred_element_type=F32)


def dot_split(value, high, low):
    value_high = value.astype(BF16)
    value_low = (value - value_high.astype(F32)).astype(BF16)
    return dot(value_high, high) + dot(value_low, high) + dot(value_high, low)


def merge_rows(value):
    blocks, rows, lanes = value.shape
    if rows % 16:
        return value.astype(F32).reshape(blocks * rows, lanes).astype(BF16)
    return value.reshape(blocks * rows, lanes)


def kernel(
    nctx,
    ntp,
    outer,
    query,
    key,
    value,
    taps_in,
    filters,
    weight_hbm,
    cot,
    ends,
    starts,
    twists,
    fwd_high,
    fwd_low,
    bwd_high,
    bwd_low,
    mixed_out,
    grad_query,
    grad_key,
    grad_value,
    grad_filters,
    grad_weight,
    weight,
    full_cot,
    cot_rows,
    taps,
    halo_out,
    halo_in,
    edge,
    shorts,
    signal,
    work,
    parts,
    spec_f,
    spec_p,
    spec_g,
    product,
    product_chan,
    conv_chan,
    conv_here,
    gated_all,
    grad_gated,
    grad_conv,
    grad_conv_chan,
    grad_chan,
    grad_here,
    shorts_grad,
    partial,
    pair_in,
    pair_sum,
    final_in,
    local_sem,
    halo_s,
    halo_r,
    cot_s,
    cot_r,
    rows_s,
    rows_r,
    quart_s,
    quart_r,
    product_s,
    product_r,
    conv_s,
    conv_r,
    grad_s,
    grad_r,
    back_s,
    back_r,
    all_s,
    all_r,
    fwd_s,
    fwd_r,
    pair_s,
    pair_r,
    final_s,
    final_r,
):
    channels, width = query.shape[1:]
    kept = nctx + 1
    tap_count = taps_in.shape[1]
    me = lax.axis_index("ctx")
    mine = lax.axis_index("tp")
    core_mate = mine + 1 - 2 * (mine % 2)
    side_mate = (mine + ntp // 2) % ntp
    far_mate = (core_mate + ntp // 2) % ntp
    x_mate = me + 1 - 2 * (me % 2)
    share = nctx // ntp
    block_rows = cot.shape[0] * cot.shape[1] * cot.shape[2]

    def send(src, dst, send_sem, recv_sem, device):
        copy = pltpu.make_async_remote_copy(
            src_ref=src,
            dst_ref=dst,
            send_sem=send_sem,
            recv_sem=recv_sem,
            device_id=device,
            device_id_type=MESH,
        )
        copy.start()
        return copy

    def peer(step):
        return lax.rem(me + step, nctx)

    def at_ctx(target):
        return (target, mine)

    def at_tp(target):
        return (me, target)

    def exchange(source, dest, send_sem, recv_sem):
        copies = []
        for step in range(1, nctx):
            target = peer(step)
            copies.append(
                send(
                    source.at[target],
                    dest.at[me],
                    send_sem.at[step],
                    recv_sem.at[step],
                    at_ctx(target),
                )
            )
        dest[me] = source[me]
        return copies

    def wait_all(copies):
        for copy in copies:
            copy.wait_recv()

    load_weight = pltpu.make_async_copy(weight_hbm, weight, local_sem)
    load_weight.start()

    barrier = pltpu.get_barrier_semaphore()
    for step in range(1, nctx):
        pl.semaphore_signal(barrier, inc=1, device_id=at_ctx(peer(step)), device_id_type=MESH)
    for mate in (core_mate, side_mate):
        pl.semaphore_signal(barrier, inc=1, device_id=at_tp(mate), device_id_type=MESH)

    def pack_edges(picks, sources):
        total = None
        for index, source in enumerate(sources):
            block = merge_rows(source[...])
            term = lax.dot_general(
                picks[index], block, (((1,), (1,)), ((), ())), preferred_element_type=F32
            )
            total = term if total is None else total + term
        halo_out[...] = total.astype(BF16)

    def unpack_edges(picks):
        for index in range(3):
            spread = lax.dot_general(
                halo_in[...], picks[index], (((0,), (0,)), ((), ())), preferred_element_type=F32
            )
            edge[index] = spread.reshape(nctx, channels, width)

    pack_edges(ends, (query, key, value))
    pl.semaphore_wait(barrier, nctx + 1)

    sent = []
    halo = send(halo_out, halo_in, halo_s.at[0], halo_r.at[0], at_ctx(peer(1)))
    own_rows = full_cot.at[pl.ds(mine * share, share)]
    to_side = send(cot, own_rows, cot_s.at[0], cot_r.at[0], at_tp(side_mate))
    to_core = send(cot, own_rows, cot_s.at[1], cot_r.at[1], at_tp(core_mate))
    sent += [to_side, to_core]
    full_cot[pl.ds(mine * share, share)] = cot[...]
    for index in range(3):
        padded = jnp.concatenate(
            [taps_in[index], jnp.zeros((taps.shape[3] - tap_count, nctx * channels), F32)], axis=0
        )
        taps[index] = padded.T.reshape(nctx, channels, taps.shape[3])

    def spectrum(spec):
        def one(k, carry):
            re = jnp.zeros((channels, width), F32)
            im = jnp.zeros((channels, width), F32)
            for n in range(nctx):
                block = signal[n]
                re = re + outer[0, k, n] * block
                im = im + outer[1, k, n] * block
            cos, sin = twists[0, k], twists[1, k]
            rows = pl.ds(pl.multiple_of(k * channels, channels), channels)
            work[rows, :width] = re * cos - im * sin
            work[rows, width:] = re * sin + im * cos
            return carry

        lax.fori_loop(0, kept, one, 0)
        spec[...] = dot_split(work[...], fwd_high[...], fwd_low[...])

    def inverse(re, im, store):
        work[:, :width] = re
        work[:, width:] = im
        work[...] = dot_split(work[...], bwd_high[...], bwd_low[...])

        def turn(k, carry):
            rows = pl.ds(pl.multiple_of(k * channels, channels), channels)
            back_re, back_im = work[rows, :width], work[rows, width:]
            cos, sin = twists[2, k], twists[3, k]
            parts[0, k] = back_re * cos + back_im * sin
            parts[1, k] = back_im * cos - back_re * sin
            return carry

        lax.fori_loop(0, kept, turn, 0)

        def one(n, carry):
            total = parts[0, 0]
            for k in range(1, kept):
                total = total + outer[0, k, n] * parts[0, k]
                if k < nctx:
                    total = total + outer[1, k, n] * parts[1, k]
            store(n, total)
            return carry

        lax.fori_loop(0, nctx, one, 0)

    lane = lax.broadcasted_iota(jnp.int32, (channels, width), 1)

    for n in range(nctx):
        signal[n] = filters[:, n * width : (n + 1) * width]
    spectrum(spec_f)

    halo.wait()
    unpack_edges(ends)
    has_before = me > 0

    def short(index):
        source = (query, key, value)[index]

        def one(m, carry):
            tap = taps[index, m]
            here = source[m].astype(F32)
            before = jnp.where(has_before, edge[index, m], 0.0)
            total = tap[:, 0:1] * here
            for j in range(1, tap_count):
                moved = pltpu.roll(jnp.where(lane >= width - j, before, here), j, 1)
                total = total + tap[:, j : j + 1] * moved
            shorts[index, m] = total.astype(BF16)
            return carry

        lax.fori_loop(0, nctx, one, 0)

    short(1)
    short(2)
    product[...] = (shorts[1].astype(F32) * shorts[2].astype(F32)).astype(BF16)
    product_copies = exchange(product, product_chan, product_s, product_r)
    sent += product_copies
    short(0)

    to_side.wait_recv()
    passed_rows = full_cot.at[pl.ds(side_mate * share, share)]
    passed = send(passed_rows, passed_rows, cot_s.at[2], cot_r.at[2], at_tp(core_mate))
    sent.append(passed)
    load_weight.wait()
    to_core.wait_recv()

    def gate_part(group):
        cot_block = full_cot[pl.ds(group * share, share)].reshape(block_rows, width)
        start = pl.multiple_of(group * block_rows, block_rows)
        return lax.dot_general(
            cot_block,
            weight[pl.ds(start, block_rows), :],
            (((0,), (0,)), ((), ())),
            preferred_element_type=F32,
        )

    total = gate_part(mine) + gate_part(core_mate) + gate_part(side_mate)
    passed.wait_recv()
    total = total + gate_part(far_mate)
    grad_gated[...] = total.T.reshape(nctx, channels, width)
    grad_conv[...] = (grad_gated[...] * shorts[0].astype(F32)).astype(BF16)
    grad_copies = exchange(grad_conv, grad_conv_chan, grad_s, grad_r)
    sent += grad_copies

    wait_all(product_copies)
    signal[...] = product_chan[...].astype(F32)
    spectrum(spec_p)

    f_re, f_im = spec_f[:, :width], spec_f[:, width:]
    p_re, p_im = spec_p[:, :width], spec_p[:, width:]

    def store_convolved(n, total):
        conv_chan[n] = total.astype(BF16)

    inverse(p_re * f_re - p_im * f_im, p_re * f_im + p_im * f_re, store_convolved)
    conv_copies = exchange(conv_chan, conv_here, conv_s, conv_r)
    sent += conv_copies

    row_copies = []
    for step in range(1, nctx):
        target = peer(step)
        row_copies.append(
            send(
                full_cot.at[target, mine],
                cot_rows.at[mine, me],
                rows_s.at[step],
                rows_r.at[step],
                at_ctx(target),
            )
        )
    sent += row_copies
    cot_rows[mine, me] = full_cot[me, mine]

    wait_all(grad_copies)
    signal[...] = grad_conv_chan[...].astype(F32)
    spectrum(spec_g)
    f_re, f_im = spec_f[:, :width], spec_f[:, width:]
    g_re, g_im = spec_g[:, :width], spec_g[:, width:]

    def store_product(n, total):
        grad_chan[n] = total.astype(BF16)

    inverse(f_re * g_re + f_im * g_im, f_re * g_im - f_im * g_re, store_product)
    back_copies = exchange(grad_chan, grad_here, back_s, back_r)
    sent += back_copies

    wait_all(conv_copies)
    gated_all[me] = (shorts[0].astype(F32) * conv_here[...].astype(F32)).astype(BF16)
    own_gated = gated_all.at[me]
    to_x = send(own_gated, own_gated, fwd_s.at[0], fwd_r.at[0], at_ctx(x_mate))
    all_copies = [
        send(own_gated, own_gated, all_s.at[step], all_r.at[step], at_ctx(peer(step)))
        for step in range(2, nctx, 2)
    ]
    sent += [to_x] + all_copies

    right = merge_rows(gated_all[me])

    def project(group):
        start = pl.multiple_of(group * block_rows, block_rows)
        return dot(weight[pl.ds(start, block_rows), :], right)

    core = mine % 2
    pair_copies = []
    for side in range(ntp // 2):
        partial[side] = project(2 * side + 1 - core).astype(BF16)
        pair_copies.append(
            send(
                partial.at[side],
                pair_in.at[side],
                pair_s.at[side],
                pair_r.at[side],
                at_tp(core_mate),
            )
        )
    sent += pair_copies

    wait_all(row_copies)
    own_quarter = cot_rows.at[mine]
    quarter_side = send(own_quarter, own_quarter, quart_s.at[0], quart_r.at[0], at_tp(side_mate))
    quarter_core = send(own_quarter, own_quarter, quart_s.at[1], quart_r.at[1], at_tp(core_mate))
    sent += [quarter_side, quarter_core]

    wait_all(back_copies)

    def gradients(m, carry):
        back = grad_here[m].astype(F32)
        shorts_grad[0, m] = (grad_gated[m] * conv_here[m].astype(F32)).astype(BF16)
        shorts_grad[1, m] = (back * shorts[2, m].astype(F32)).astype(BF16)
        shorts_grad[2, m] = (back * shorts[1, m].astype(F32)).astype(BF16)
        return carry

    lax.fori_loop(0, nctx, gradients, 0)
    pack_edges(starts, [shorts_grad.at[index] for index in range(3)])
    halo = send(halo_out, halo_in, halo_s.at[1], halo_r.at[1], at_ctx(peer(nctx - 1)))

    my_side = mine // 2
    wait_all(pair_copies)
    pair_sum[...] = (project(side_mate) + pair_in[1 - my_side].astype(F32)).astype(BF16)
    final = send(pair_sum, final_in, final_s, final_r, at_tp(side_mate))
    sent.append(final)

    def pass_on(copy, step):
        copy.wait_recv()
        block = gated_all.at[peer(nctx - step)]
        slot = step // 2
        return send(block, block, fwd_s.at[slot], fwd_r.at[slot], at_ctx(x_mate))

    steps = list(range(2, nctx, 2))
    passed_all = [pass_on(all_copies[0], steps[0])]

    halo.wait()
    unpack_edges(starts)
    has_after = me < nctx - 1
    for index, result in enumerate((grad_query, grad_key, grad_value)):

        def long(m, carry, index=index, result=result):
            tap = taps[index, m]
            here = shorts_grad[index, m].astype(F32)
            after = jnp.where(has_after, edge[index, m], 0.0)
            total = tap[:, 0:1] * here
            for j in range(1, tap_count):
                moved = pltpu.roll(jnp.where(lane < j, after, here), width - j, 1)
                total = total + tap[:, j : j + 1] * moved
            result[m] = total.astype(BF16)
            return carry

        lax.fori_loop(0, nctx, long, 0)

    for copy, step in zip(all_copies[1:], steps[1:]):
        passed_all.append(pass_on(copy, step))
    sent += passed_all
    quarter_side.wait_recv()
    far_quarter = cot_rows.at[side_mate]
    quarter_far = send(far_quarter, far_quarter, quart_s.at[2], quart_r.at[2], at_tp(core_mate))
    sent.append(quarter_far)

    p_re, p_im = spec_p[:, :width], spec_p[:, width:]
    g_re, g_im = spec_g[:, :width], spec_g[:, width:]

    def store_filters(n, total):
        grad_filters[:, pl.ds(pl.multiple_of(n * width, width), width)] = total

    inverse(p_re * g_re + p_im * g_im, p_re * g_im - p_im * g_re, store_filters)

    own_sum = project(mine) + pair_in[my_side].astype(F32)
    final.wait_recv()
    mixed_out[...] = (own_sum + final_in[...].astype(F32)).astype(BF16)

    quarter_core.wait_recv()
    quarter_far.wait_recv()
    quarter = cot_rows.shape[2]

    def weigh(n):
        return lax.dot_general(
            cot_rows[:, n].reshape(ntp * quarter, width),
            merge_rows(gated_all[n]),
            (((1,), (1,)), ((), ())),
            preferred_element_type=F32,
        )

    grad_weight[...] = weigh(me)
    for step in steps:
        grad_weight[...] += weigh(peer(nctx - step))
    to_x.wait_recv()
    grad_weight[...] += weigh(x_mate)
    for copy, step in zip(passed_all, steps):
        copy.wait_recv()
        grad_weight[...] += weigh(lax.rem(x_mate + nctx - step, nctx))

    for copy in sent:
        copy.wait_send()


def hand_on(*refs):
    count = len(refs) // 2
    sources, dests, sem = refs[:count], refs[count:-1], refs[-1]
    copies = [
        pltpu.make_async_copy(source, dest, sem.at[index])
        for index, (source, dest) in enumerate(zip(sources, dests))
    ]
    for copy in copies:
        copy.start()
    for copy in copies:
        copy.wait()


def per_device(nctx, ntp, query_in, key_in, value_in, short_weights, filters, out_weight, cotangent):
    rows, width = query_in.shape
    channels = rows // nctx
    features = out_weight.shape[0]
    quarter = features // (nctx * ntp)
    share = nctx // ntp
    kept = nctx + 1
    outer, twists, *inner = make_tables(nctx, width)
    tap_count = short_weights.shape[2]
    tap_slots = -(-tap_count // 8) * 8
    edge_rows = -(-3 * tap_slots // 16) * 16
    ends = np.zeros((3, edge_rows, width), np.float32)
    starts = np.zeros((3, edge_rows, width), np.float32)
    for index in range(3):
        for j in range(tap_count - 1):
            ends[index, index * tap_slots + j, width - (tap_count - 1) + j] = 1.0
            starts[index, index * tap_slots + j, j] = 1.0
    blocks = (nctx, channels, width)

    def bf(*shape):
        return pltpu.VMEM(shape, BF16)

    def f32(*shape):
        return pltpu.VMEM(shape, F32)

    def sems(*shape):
        return pltpu.SemaphoreType.DMA(shape)

    vmem = pl.BlockSpec(memory_space=pltpu.VMEM)
    smem = pl.BlockSpec(memory_space=pltpu.SMEM)
    anywhere = pl.BlockSpec(memory_space=pl.ANY)
    out_shape = (
        jax.ShapeDtypeStruct((features // ntp, width), BF16),
        jax.ShapeDtypeStruct(blocks, BF16),
        jax.ShapeDtypeStruct(blocks, BF16),
        jax.ShapeDtypeStruct(blocks, BF16),
        jax.ShapeDtypeStruct((channels, nctx * width), F32),
        jax.ShapeDtypeStruct((features // nctx, rows), F32),
    )
    outs = pl.pallas_call(
        functools.partial(kernel, nctx, ntp),
        out_shape=out_shape,
        in_specs=[smem] + [vmem] * 5 + [anywhere] + [vmem] * 8,
        out_specs=tuple([vmem] * 6),
        scratch_shapes=[
            bf(features, rows),
            bf(nctx, ntp, quarter, width),
            bf(ntp, nctx, quarter, width),
            f32(3, nctx, channels, tap_slots),
            bf(edge_rows, rows),
            bf(edge_rows, rows),
            f32(3, *blocks),
            bf(3, *blocks),
            f32(*blocks),
            f32(kept * channels, 2 * width),
            f32(2, kept, channels, width),
            f32(kept * channels, 2 * width),
            f32(kept * channels, 2 * width),
            f32(kept * channels, 2 * width),
            bf(*blocks),
            bf(*blocks),
            bf(*blocks),
            bf(*blocks),
            bf(nctx, *blocks),
            f32(*blocks),
            bf(*blocks),
            bf(*blocks),
            bf(*blocks),
            bf(*blocks),
            bf(3, *blocks),
            bf(ntp // 2, features // ntp, width),
            bf(ntp // 2, features // ntp, width),
            bf(features // ntp, width),
            bf(features // ntp, width),
            pltpu.SemaphoreType.DMA,
            sems(2),
            sems(2),
            sems(3),
            sems(3),
            sems(nctx),
            sems(nctx),
            sems(3),
            sems(3),
            sems(nctx),
            sems(nctx),
            sems(nctx),
            sems(nctx),
            sems(nctx),
            sems(nctx),
            sems(nctx),
            sems(nctx),
            sems(nctx),
            sems(nctx),
            sems(nctx),
            sems(nctx),
            sems(ntp // 2),
            sems(ntp // 2),
            pltpu.SemaphoreType.DMA,
            pltpu.SemaphoreType.DMA,
        ],
        compiler_params=pltpu.CompilerParams(
            collective_id=0, has_side_effects=True, vmem_limit_bytes=56 * 1024 * 1024
        ),
        cost_estimate=pl.CostEstimate(
            flops=6 * features * rows * width, bytes_accessed=10 * features * rows // 4, transcendentals=0
        ),
        name="mixer",
    )(
        jnp.asarray(outer),
        query_in.reshape(blocks),
        key_in.reshape(blocks),
        value_in.reshape(blocks),
        short_weights.transpose(0, 2, 1),
        filters.reshape(channels, nctx * width),
        out_weight,
        cotangent.reshape(share, ntp, quarter, width),
        jnp.asarray(ends.astype(jnp.bfloat16)),
        jnp.asarray(starts.astype(jnp.bfloat16)),
        jnp.asarray(twists),
        *[jnp.asarray(table) for table in inner],
    )
    outs = pl.pallas_call(
        hand_on,
        out_shape=out_shape,
        in_specs=[anywhere] * 6,
        out_specs=tuple([anywhere] * 6),
        scratch_shapes=[sems(6)],
        name="hand_on",
    )(*outs)
    mixed, grad_query, grad_key, grad_value, grad_filters, grad_weight = outs
    return (
        mixed,
        grad_query.reshape(rows, width),
        grad_key.reshape(rows, width),
        grad_value.reshape(rows, width),
        grad_filters.reshape(filters.shape),
        grad_weight,
    )


def solution(mesh):
    placed = (
        P("tp", "ctx"),
        P("tp", "ctx"),
        P("tp", "ctx"),
        P(None, "tp", None),
        P("tp", "ctx", None),
        P(None, "tp"),
        P("tp", "ctx"),
    )
    return jax.shard_map(
        functools.partial(per_device, mesh.shape["ctx"], mesh.shape["tp"]),
        mesh=mesh,
        in_specs=placed,
        out_specs=(
            P("tp", "ctx"),
            P("tp", "ctx"),
            P("tp", "ctx"),
            P("tp", "ctx"),
            P("tp", "ctx", None),
            P("ctx", "tp"),
        ),
        check_vma=False,
    )
```

```python
import functools

import jax
import jax.numpy as jnp
import numpy as np
from jax import lax
from jax.experimental import pallas as pl
from jax.experimental.pallas import tpu as pltpu
from jax.sharding import PartitionSpec as P

F32 = jnp.float32
BF16 = jnp.bfloat16
MESH = pl.DeviceIdType.MESH


def split_table(table):
    table = table.astype(np.float32)
    high = table.astype(jnp.bfloat16)
    low = (table - high.astype(np.float32)).astype(jnp.bfloat16)
    return high, low


def make_tables(blocks, width):
    rows = 2 * blocks
    full = rows * width
    kept = blocks + 1
    turn = np.outer(np.arange(kept), np.arange(blocks)) % rows * (2 * np.pi / rows)
    outer = np.stack([np.cos(turn), -np.sin(turn)]).astype(np.float32)
    twist = np.outer(np.arange(kept), np.arange(width)) % full * (2 * np.pi / full)
    weight = np.full((kept, 1), 2.0 / full)
    weight[0] = weight[-1] = 1.0 / full
    twists = np.stack(
        [np.cos(twist), -np.sin(twist), weight * np.cos(twist), weight * -np.sin(twist)]
    ).astype(np.float32)[:, :, None, :]
    inner = np.outer(np.arange(width), np.arange(width)) % width * (2 * np.pi / width)
    re, im = np.cos(inner), -np.sin(inner)
    forward = np.block([[re, im], [-im, re]])
    backward = np.block([[re, -im], [im, re]])
    return outer, twists, *split_table(forward), *split_table(backward)


def dot(a, b):
    return jnp.dot(a, b, preferred_element_type=F32)


def dot_split(value, high, low):
    value_high = value.astype(BF16)
    value_low = (value - value_high.astype(F32)).astype(BF16)
    return dot(value_high, high) + dot(value_low, high) + dot(value_high, low)


def merge_rows(value):
    blocks, rows, lanes = value.shape
    if rows % 16:
        return value.astype(F32).reshape(blocks * rows, lanes).astype(BF16)
    return value.reshape(blocks * rows, lanes)


def kernel(
    nctx,
    ntp,
    outer,
    query,
    key,
    value,
    taps_in,
    filters,
    weight_hbm,
    cot,
    ends,
    starts,
    twists,
    fwd_high,
    fwd_low,
    bwd_high,
    bwd_low,
    mixed_out,
    grad_query,
    grad_key,
    grad_value,
    grad_filters,
    grad_weight,
    weight,
    full_cot,
    cot_rows,
    taps,
    halo_out,
    halo_in,
    edge,
    shorts,
    signal,
    work,
    parts,
    spec_f,
    spec_p,
    spec_g,
    product,
    product_chan,
    conv_chan,
    conv_here,
    gated_all,
    grad_gated,
    grad_conv,
    grad_conv_chan,
    grad_chan,
    grad_here,
    shorts_grad,
    partial,
    pair_in,
    pair_sum,
    final_in,
    local_sem,
    halo_s,
    halo_r,
    cot_s,
    cot_r,
    rows_s,
    rows_r,
    quart_s,
    quart_r,
    product_s,
    product_r,
    conv_s,
    conv_r,
    grad_s,
    grad_r,
    back_s,
    back_r,
    all_s,
    all_r,
    fwd_s,
    fwd_r,
    pair_s,
    pair_r,
    final_s,
    final_r,
):
    channels, width = query.shape[1:]
    kept = nctx + 1
    tap_count = taps_in.shape[1]
    me = lax.axis_index("ctx")
    mine = lax.axis_index("tp")
    core_mate = mine + 1 - 2 * (mine % 2)
    side_mate = (mine + ntp // 2) % ntp
    far_mate = (core_mate + ntp // 2) % ntp
    x_mate = me + 1 - 2 * (me % 2)
    share = nctx // ntp
    block_rows = cot.shape[0] * cot.shape[1] * cot.shape[2]

    def send(src, dst, send_sem, recv_sem, device):
        copy = pltpu.make_async_remote_copy(
            src_ref=src,
            dst_ref=dst,
            send_sem=send_sem,
            recv_sem=recv_sem,
            device_id=device,
            device_id_type=MESH,
        )
        copy.start()
        return copy

    def peer(step):
        return lax.rem(me + step, nctx)

    def at_ctx(target):
        return (target, mine)

    def at_tp(target):
        return (me, target)

    def exchange(source, dest, send_sem, recv_sem):
        copies = []
        for step in range(1, nctx):
            target = peer(step)
            copies.append(
                send(
                    source.at[target],
                    dest.at[me],
                    send_sem.at[step],
                    recv_sem.at[step],
                    at_ctx(target),
                )
            )
        dest[me] = source[me]
        return copies

    def wait_all(copies):
        for copy in copies:
            copy.wait_recv()

    load_weight = pltpu.make_async_copy(weight_hbm, weight, local_sem)
    load_weight.start()

    barrier = pltpu.get_barrier_semaphore()
    for step in range(1, nctx):
        pl.semaphore_signal(barrier, inc=1, device_id=at_ctx(peer(step)), device_id_type=MESH)
    for mate in (core_mate, side_mate):
        pl.semaphore_signal(barrier, inc=1, device_id=at_tp(mate), device_id_type=MESH)

    def pack_edges(picks, sources):
        total = None
        for index, source in enumerate(sources):
            block = merge_rows(source[...])
            term = lax.dot_general(
                picks[index], block, (((1,), (1,)), ((), ())), preferred_element_type=F32
            )
            total = term if total is None else total + term
        halo_out[...] = total.astype(BF16)

    def unpack_edges(picks):
        for index in range(3):
            spread = lax.dot_general(
                halo_in[...], picks[index], (((0,), (0,)), ((), ())), preferred_element_type=F32
            )
            edge[index] = spread.reshape(nctx, channels, width)

    pack_edges(ends, (query, key, value))
    pl.semaphore_wait(barrier, nctx + 1)

    sent = []
    halo = send(halo_out, halo_in, halo_s.at[0], halo_r.at[0], at_ctx(peer(1)))
    own_rows = full_cot.at[pl.ds(mine * share, share)]
    to_side = send(cot, own_rows, cot_s.at[0], cot_r.at[0], at_tp(side_mate))
    to_core = send(cot, own_rows, cot_s.at[1], cot_r.at[1], at_tp(core_mate))
    sent += [to_side, to_core]
    full_cot[pl.ds(mine * share, share)] = cot[...]
    for index in range(3):
        padded = jnp.concatenate(
            [taps_in[index], jnp.zeros((taps.shape[3] - tap_count, nctx * channels), F32)], axis=0
        )
        taps[index] = padded.T.reshape(nctx, channels, taps.shape[3])

    def spectrum(spec):
        def one(k, carry):
            re = jnp.zeros((channels, width), F32)
            im = jnp.zeros((channels, width), F32)
            for n in range(nctx):
                block = signal[n]
                re = re + outer[0, k, n] * block
                im = im + outer[1, k, n] * block
            cos, sin = twists[0, k], twists[1, k]
            rows = pl.ds(pl.multiple_of(k * channels, channels), channels)
            work[rows, :width] = re * cos - im * sin
            work[rows, width:] = re * sin + im * cos
            return carry

        lax.fori_loop(0, kept, one, 0)
        spec[...] = dot_split(work[...], fwd_high[...], fwd_low[...])

    def inverse(re, im, store):
        work[:, :width] = re
        work[:, width:] = im
        work[...] = dot_split(work[...], bwd_high[...], bwd_low[...])

        def turn(k, carry):
            rows = pl.ds(pl.multiple_of(k * channels, channels), channels)
            back_re, back_im = work[rows, :width], work[rows, width:]
            cos, sin = twists[2, k], twists[3, k]
            parts[0, k] = back_re * cos + back_im * sin
            parts[1, k] = back_im * cos - back_re * sin
            return carry

        lax.fori_loop(0, kept, turn, 0)

        def one(n, carry):
            total = parts[0, 0]
            for k in range(1, kept):
                total = total + outer[0, k, n] * parts[0, k]
                if k < nctx:
                    total = total + outer[1, k, n] * parts[1, k]
            store(n, total)
            return carry

        lax.fori_loop(0, nctx, one, 0)

    lane = lax.broadcasted_iota(jnp.int32, (channels, width), 1)

    for n in range(nctx):
        signal[n] = filters[:, n * width : (n + 1) * width]
    spectrum(spec_f)

    halo.wait()
    unpack_edges(ends)
    has_before = me > 0

    def short(index):
        source = (query, key, value)[index]

        def one(m, carry):
            tap = taps[index, m]
            here = source[m].astype(F32)
            before = jnp.where(has_before, edge[index, m], 0.0)
            total = tap[:, 0:1] * here
            for j in range(1, tap_count):
                moved = pltpu.roll(jnp.where(lane >= width - j, before, here), j, 1)
                total = total + tap[:, j : j + 1] * moved
            shorts[index, m] = total.astype(BF16)
            return carry

        lax.fori_loop(0, nctx, one, 0)

    short(1)
    short(2)
    product[...] = (shorts[1].astype(F32) * shorts[2].astype(F32)).astype(BF16)
    product_copies = exchange(product, product_chan, product_s, product_r)
    sent += product_copies
    short(0)

    to_side.wait_recv()
    passed_rows = full_cot.at[pl.ds(side_mate * share, share)]
    passed = send(passed_rows, passed_rows, cot_s.at[2], cot_r.at[2], at_tp(core_mate))
    sent.append(passed)
    load_weight.wait()
    to_core.wait_recv()

    def gate_part(group):
        cot_block = full_cot[pl.ds(group * share, share)].reshape(block_rows, width)
        start = pl.multiple_of(group * block_rows, block_rows)
        return lax.dot_general(
            cot_block,
            weight[pl.ds(start, block_rows), :],
            (((0,), (0,)), ((), ())),
            preferred_element_type=F32,
        )

    total = gate_part(mine) + gate_part(core_mate) + gate_part(side_mate)
    passed.wait_recv()
    total = total + gate_part(far_mate)
    grad_gated[...] = total.T.reshape(nctx, channels, width)
    grad_conv[...] = (grad_gated[...] * shorts[0].astype(F32)).astype(BF16)
    grad_copies = exchange(grad_conv, grad_conv_chan, grad_s, grad_r)
    sent += grad_copies

    wait_all(product_copies)
    signal[...] = product_chan[...].astype(F32)
    spectrum(spec_p)

    f_re, f_im = spec_f[:, :width], spec_f[:, width:]
    p_re, p_im = spec_p[:, :width], spec_p[:, width:]

    def store_convolved(n, total):
        conv_chan[n] = total.astype(BF16)

    inverse(p_re * f_re - p_im * f_im, p_re * f_im + p_im * f_re, store_convolved)
    conv_copies = exchange(conv_chan, conv_here, conv_s, conv_r)
    sent += conv_copies

    row_copies = []
    for step in range(1, nctx):
        target = peer(step)
        row_copies.append(
            send(
                full_cot.at[target, mine],
                cot_rows.at[mine, me],
                rows_s.at[step],
                rows_r.at[step],
                at_ctx(target),
            )
        )
    sent += row_copies
    cot_rows[mine, me] = full_cot[me, mine]

    wait_all(grad_copies)
    signal[...] = grad_conv_chan[...].astype(F32)
    spectrum(spec_g)
    f_re, f_im = spec_f[:, :width], spec_f[:, width:]
    g_re, g_im = spec_g[:, :width], spec_g[:, width:]

    def store_product(n, total):
        grad_chan[n] = total.astype(BF16)

    inverse(f_re * g_re + f_im * g_im, f_re * g_im - f_im * g_re, store_product)
    back_copies = exchange(grad_chan, grad_here, back_s, back_r)
    sent += back_copies

    wait_all(conv_copies)
    gated_all[me] = (shorts[0].astype(F32) * conv_here[...].astype(F32)).astype(BF16)
    line = nctx // 2
    place = me // 2

    def relay(step, way, action):
        sign = 1 - 2 * way
        block = gated_all.at[me - sign * 2 * step]
        return pltpu.make_async_remote_copy(
            src_ref=block,
            dst_ref=block,
            send_sem=all_s.at[way, step],
            recv_sem=all_r.at[way, step + 1 - action],
            device_id=at_ctx(me + sign * (2 - 4 * action)),
            device_id_type=MESH,
        )

    def came(step, way):
        return place >= step if way == 0 else place < line - step

    def goes(step, way):
        more = place < line - 1 if way == 0 else place > 0
        return more if step == 0 else jnp.logical_and(came(step, way), more)

    def to_mate(spot):
        block = gated_all.at[2 * spot + me % 2]
        return pltpu.make_async_remote_copy(
            src_ref=block,
            dst_ref=block,
            send_sem=fwd_s.at[spot],
            recv_sem=fwd_r.at[spot],
            device_id=at_ctx(x_mate),
            device_id_type=MESH,
        )

    def pass_on(step):
        for way in range(2):
            if step:

                @pl.when(came(step, way))
                def _():
                    relay(step, way, 1).wait_recv()

            if step < line - 1:

                @pl.when(goes(step, way))
                def _():
                    relay(step, way, 0).start()

            if step:

                @pl.when(came(step, way))
                def _():
                    to_mate(place - step * (1 - 2 * way)).start()

        if step == 0:
            to_mate(place).start()

    pass_on(0)

    right = merge_rows(gated_all[me])

    def project(group):
        start = pl.multiple_of(group * block_rows, block_rows)
        return dot(weight[pl.ds(start, block_rows), :], right)

    core = mine % 2
    pair_copies = []
    for side in range(ntp // 2):
        partial[side] = project(2 * side + 1 - core).astype(BF16)
        pair_copies.append(
            send(
                partial.at[side],
                pair_in.at[side],
                pair_s.at[side],
                pair_r.at[side],
                at_tp(core_mate),
            )
        )
    sent += pair_copies

    wait_all(row_copies)
    own_quarter = cot_rows.at[mine]
    quarter_side = send(own_quarter, own_quarter, quart_s.at[0], quart_r.at[0], at_tp(side_mate))
    quarter_core = send(own_quarter, own_quarter, quart_s.at[1], quart_r.at[1], at_tp(core_mate))
    sent += [quarter_side, quarter_core]

    wait_all(back_copies)

    def gradients(m, carry):
        back = grad_here[m].astype(F32)
        shorts_grad[0, m] = (grad_gated[m] * conv_here[m].astype(F32)).astype(BF16)
        shorts_grad[1, m] = (back * shorts[2, m].astype(F32)).astype(BF16)
        shorts_grad[2, m] = (back * shorts[1, m].astype(F32)).astype(BF16)
        return carry

    lax.fori_loop(0, nctx, gradients, 0)
    pack_edges(starts, [shorts_grad.at[index] for index in range(3)])
    halo = send(halo_out, halo_in, halo_s.at[1], halo_r.at[1], at_ctx(peer(nctx - 1)))

    my_side = mine // 2
    wait_all(pair_copies)
    pair_sum[...] = (project(side_mate) + pair_in[1 - my_side].astype(F32)).astype(BF16)
    final = send(pair_sum, final_in, final_s, final_r, at_tp(side_mate))
    sent.append(final)

    for step in range(1, line - 1):
        pass_on(step)

    halo.wait()
    unpack_edges(starts)
    has_after = me < nctx - 1
    for index, result in enumerate((grad_query, grad_key, grad_value)):

        def long(m, carry, index=index, result=result):
            tap = taps[index, m]
            here = shorts_grad[index, m].astype(F32)
            after = jnp.where(has_after, edge[index, m], 0.0)
            total = tap[:, 0:1] * here
            for j in range(1, tap_count):
                moved = pltpu.roll(jnp.where(lane < j, after, here), width - j, 1)
                total = total + tap[:, j : j + 1] * moved
            result[m] = total.astype(BF16)
            return carry

        lax.fori_loop(0, nctx, long, 0)

    pass_on(line - 1)
    quarter_side.wait_recv()
    far_quarter = cot_rows.at[side_mate]
    quarter_far = send(far_quarter, far_quarter, quart_s.at[2], quart_r.at[2], at_tp(core_mate))
    sent.append(quarter_far)

    p_re, p_im = spec_p[:, :width], spec_p[:, width:]
    g_re, g_im = spec_g[:, :width], spec_g[:, width:]

    def store_filters(n, total):
        grad_filters[:, pl.ds(pl.multiple_of(n * width, width), width)] = total

    inverse(p_re * g_re + p_im * g_im, p_re * g_im - p_im * g_re, store_filters)

    own_sum = project(mine) + pair_in[my_side].astype(F32)
    final.wait_recv()
    mixed_out[...] = (own_sum + final_in[...].astype(F32)).astype(BF16)

    quarter_core.wait_recv()
    quarter_far.wait_recv()
    quarter = cot_rows.shape[2]

    def weigh(column):
        left = [
            cot_rows[:, 2 * spot + column].reshape(ntp * quarter, width) for spot in range(line)
        ]
        right = [merge_rows(gated_all[2 * spot + column]) for spot in range(line)]
        return lax.dot_general(
            jnp.concatenate(left, axis=1),
            jnp.concatenate(right, axis=1),
            (((1,), (1,)), ((), ())),
            preferred_element_type=F32,
        )

    grad_weight[...] = weigh(me % 2)
    for spot in range(line):
        to_mate(spot).wait_recv()
    grad_weight[...] += weigh(x_mate % 2)

    for copy in sent:
        copy.wait_send()
    for spot in range(line):
        to_mate(spot).wait_send()
    for step in range(line - 1):
        for way in range(2):

            @pl.when(goes(step, way))
            def _(step=step, way=way):
                relay(step, way, 0).wait_send()


def hand_on(*refs):
    count = len(refs) // 2
    for source, dest in zip(refs[:count], refs[count:]):
        dest[...] = source[...]


def per_device(nctx, ntp, query_in, key_in, value_in, short_weights, filters, out_weight, cotangent):
    rows, width = query_in.shape
    channels = rows // nctx
    features = out_weight.shape[0]
    quarter = features // (nctx * ntp)
    share = nctx // ntp
    kept = nctx + 1
    outer, twists, *inner = make_tables(nctx, width)
    tap_count = short_weights.shape[2]
    tap_slots = -(-tap_count // 8) * 8
    edge_rows = -(-3 * tap_slots // 16) * 16
    ends = np.zeros((3, edge_rows, width), np.float32)
    starts = np.zeros((3, edge_rows, width), np.float32)
    for index in range(3):
        for j in range(tap_count - 1):
            ends[index, index * tap_slots + j, width - (tap_count - 1) + j] = 1.0
            starts[index, index * tap_slots + j, j] = 1.0
    blocks = (nctx, channels, width)

    def bf(*shape):
        return pltpu.VMEM(shape, BF16)

    def f32(*shape):
        return pltpu.VMEM(shape, F32)

    def sems(*shape):
        return pltpu.SemaphoreType.DMA(shape)

    vmem = pl.BlockSpec(memory_space=pltpu.VMEM)
    smem = pl.BlockSpec(memory_space=pltpu.SMEM)
    anywhere = pl.BlockSpec(memory_space=pl.ANY)
    out_shape = (
        jax.ShapeDtypeStruct((features // ntp, width), BF16),
        jax.ShapeDtypeStruct(blocks, BF16),
        jax.ShapeDtypeStruct(blocks, BF16),
        jax.ShapeDtypeStruct(blocks, BF16),
        jax.ShapeDtypeStruct((channels, nctx * width), F32),
        jax.ShapeDtypeStruct((features // nctx, rows), F32),
    )
    outs = pl.pallas_call(
        functools.partial(kernel, nctx, ntp),
        out_shape=out_shape,
        in_specs=[smem] + [vmem] * 5 + [anywhere] + [vmem] * 8,
        out_specs=tuple([vmem] * 6),
        scratch_shapes=[
            bf(features, rows),
            bf(nctx, ntp, quarter, width),
            bf(ntp, nctx, quarter, width),
            f32(3, nctx, channels, tap_slots),
            bf(edge_rows, rows),
            bf(edge_rows, rows),
            f32(3, *blocks),
            bf(3, *blocks),
            f32(*blocks),
            f32(kept * channels, 2 * width),
            f32(2, kept, channels, width),
            f32(kept * channels, 2 * width),
            f32(kept * channels, 2 * width),
            f32(kept * channels, 2 * width),
            bf(*blocks),
            bf(*blocks),
            bf(*blocks),
            bf(*blocks),
            bf(nctx, *blocks),
            f32(*blocks),
            bf(*blocks),
            bf(*blocks),
            bf(*blocks),
            bf(*blocks),
            bf(3, *blocks),
            bf(ntp // 2, features // ntp, width),
            bf(ntp // 2, features // ntp, width),
            bf(features // ntp, width),
            bf(features // ntp, width),
            pltpu.SemaphoreType.DMA,
            sems(2),
            sems(2),
            sems(3),
            sems(3),
            sems(nctx),
            sems(nctx),
            sems(3),
            sems(3),
            sems(nctx),
            sems(nctx),
            sems(nctx),
            sems(nctx),
            sems(nctx),
            sems(nctx),
            sems(nctx),
            sems(nctx),
            sems(2, nctx // 2),
            sems(2, nctx // 2),
            sems(nctx),
            sems(nctx),
            sems(ntp // 2),
            sems(ntp // 2),
            pltpu.SemaphoreType.DMA,
            pltpu.SemaphoreType.DMA,
        ],
        compiler_params=pltpu.CompilerParams(
            collective_id=0, has_side_effects=True, vmem_limit_bytes=56 * 1024 * 1024
        ),
        cost_estimate=pl.CostEstimate(
            flops=6 * features * rows * width, bytes_accessed=10 * features * rows // 4, transcendentals=0
        ),
        name="mixer",
    )(
        jnp.asarray(outer),
        query_in.reshape(blocks),
        key_in.reshape(blocks),
        value_in.reshape(blocks),
        short_weights.transpose(0, 2, 1),
        filters.reshape(channels, nctx * width),
        out_weight,
        cotangent.reshape(share, ntp, quarter, width),
        jnp.asarray(ends.astype(jnp.bfloat16)),
        jnp.asarray(starts.astype(jnp.bfloat16)),
        jnp.asarray(twists),
        *[jnp.asarray(table) for table in inner],
    )
    outs = pl.pallas_call(
        hand_on,
        out_shape=out_shape,
        in_specs=[vmem] * 6,
        out_specs=tuple([vmem] * 6),
        compiler_params=pltpu.CompilerParams(vmem_limit_bytes=16 * 1024 * 1024),
        name="hand_on",
    )(*outs)
    mixed, grad_query, grad_key, grad_value, grad_filters, grad_weight = outs
    return (
        mixed,
        grad_query.reshape(rows, width),
        grad_key.reshape(rows, width),
        grad_value.reshape(rows, width),
        grad_filters.reshape(filters.shape),
        grad_weight,
    )


def solution(mesh):
    placed = (
        P("tp", "ctx"),
        P("tp", "ctx"),
        P("tp", "ctx"),
        P(None, "tp", None),
        P("tp", "ctx", None),
        P(None, "tp"),
        P("tp", "ctx"),
    )
    return jax.shard_map(
        functools.partial(per_device, mesh.shape["ctx"], mesh.shape["tp"]),
        mesh=mesh,
        in_specs=placed,
        out_specs=(
            P("tp", "ctx"),
            P("tp", "ctx"),
            P("tp", "ctx"),
            P("tp", "ctx"),
            P("tp", "ctx", None),
            P("ctx", "tp"),
        ),
        check_vma=False,
    )
```

```python
import functools

import jax
import jax.numpy as jnp
import numpy as np
from jax import lax
from jax.experimental import pallas as pl
from jax.experimental.pallas import tpu as pltpu
from jax.sharding import PartitionSpec as P

F32 = jnp.float32
BF16 = jnp.bfloat16
MESH = pl.DeviceIdType.MESH


def split_table(table):
    table = table.astype(np.float32)
    high = table.astype(jnp.bfloat16)
    low = (table - high.astype(np.float32)).astype(jnp.bfloat16)
    return high, low


def make_tables(blocks, width):
    rows = 2 * blocks
    full = rows * width
    kept = blocks + 1
    turn = np.outer(np.arange(kept), np.arange(blocks)) % rows * (2 * np.pi / rows)
    outer = np.stack([np.cos(turn), -np.sin(turn)]).astype(np.float32)
    twist = np.outer(np.arange(kept), np.arange(width)) % full * (2 * np.pi / full)
    weight = np.full((kept, 1), 2.0 / full)
    weight[0] = weight[-1] = 1.0 / full
    twists = np.stack(
        [np.cos(twist), -np.sin(twist), weight * np.cos(twist), weight * -np.sin(twist)]
    ).astype(np.float32)[:, :, None, :]
    inner = np.outer(np.arange(width), np.arange(width)) % width * (2 * np.pi / width)
    re, im = np.cos(inner), -np.sin(inner)
    forward = np.block([[re, im], [-im, re]])
    backward = np.block([[re, -im], [im, re]])
    return outer, twists, *split_table(forward), *split_table(backward)


def dot(a, b):
    return jnp.dot(a, b, preferred_element_type=F32)


def dot_split(value, high, low):
    value_high = value.astype(BF16)
    value_low = (value - value_high.astype(F32)).astype(BF16)
    return dot(value_high, high) + dot(value_low, high) + dot(value_high, low)


def merge_rows(value):
    blocks, rows, lanes = value.shape
    if rows % 16:
        return value.astype(F32).reshape(blocks * rows, lanes).astype(BF16)
    return value.reshape(blocks * rows, lanes)


INPUTS = 14
OUTPUTS = 6


def kernel(nctx, ntp, outer, *refs):
    given, refs = refs[:INPUTS], refs[INPUTS:]
    wanted, refs = refs[:OUTPUTS], refs[OUTPUTS:]
    held, refs = refs[:INPUTS], refs[INPUTS:]
    made, refs = refs[:OUTPUTS], refs[OUTPUTS:]
    in_sem, out_sem, *refs = refs
    loads = {}
    for index in (0, 1, 2, 7, 6, 3, 4, 9, 10, 11, 12, 13, 8, 5):
        loads[index] = pltpu.make_async_copy(given[index], held[index], in_sem.at[index])
        loads[index].start()

    def loaded(*indices):
        for index in indices:
            loads[index].wait()

    stores = []

    def store(index, rows=None, slot=None):
        source, dest = made[index], wanted[index]
        if rows is not None:
            source, dest = source.at[rows], dest.at[rows]
        copy = pltpu.make_async_copy(source, dest, out_sem.at[index if slot is None else slot])
        copy.start()
        stores.append(copy)

    (
        query,
        key,
        value,
        taps_in,
        filters,
        weight,
        cot,
        ends,
        starts,
        twists,
        fwd_high,
        fwd_low,
        bwd_high,
        bwd_low,
    ) = held
    (
        mixed_out,
        grad_query,
        grad_key,
        grad_value,
        grad_filters,
        grad_weight,
    ) = made
    (
        full_cot,
        cot_rows,
        taps,
        halo_out,
        halo_in,
        edge,
        shorts,
        signal,
        work,
        parts,
        spec_f,
        spec_p,
        spec_g,
        product,
        product_chan,
        conv_chan,
        conv_here,
        gated_all,
        grad_gated,
        grad_conv,
        grad_conv_chan,
        grad_chan,
        grad_here,
        shorts_grad,
        partial,
        pair_in,
        pair_sum,
        final_in,
        halo_s,
        halo_r,
        cot_s,
        cot_r,
        rows_s,
        rows_r,
        quart_s,
        quart_r,
        product_s,
        product_r,
        conv_s,
        conv_r,
        grad_s,
        grad_r,
        back_s,
        back_r,
        all_s,
        all_r,
        fwd_s,
        fwd_r,
        pair_s,
        pair_r,
        final_s,
        final_r,
    ) = refs
    channels, width = query.shape[1:]
    kept = nctx + 1
    tap_count = taps_in.shape[1]
    me = lax.axis_index("ctx")
    mine = lax.axis_index("tp")
    core_mate = mine + 1 - 2 * (mine % 2)
    side_mate = (mine + ntp // 2) % ntp
    far_mate = (core_mate + ntp // 2) % ntp
    x_mate = me + 1 - 2 * (me % 2)
    share = nctx // ntp
    block_rows = cot.shape[0] * cot.shape[1] * cot.shape[2]

    def send(src, dst, send_sem, recv_sem, device):
        copy = pltpu.make_async_remote_copy(
            src_ref=src,
            dst_ref=dst,
            send_sem=send_sem,
            recv_sem=recv_sem,
            device_id=device,
            device_id_type=MESH,
        )
        copy.start()
        return copy

    def peer(step):
        return lax.rem(me + step, nctx)

    def at_ctx(target):
        return (target, mine)

    def at_tp(target):
        return (me, target)

    def exchange(source, dest, send_sem, recv_sem):
        copies = []
        for step in range(1, nctx):
            target = peer(step)
            copies.append(
                send(
                    source.at[target],
                    dest.at[me],
                    send_sem.at[step],
                    recv_sem.at[step],
                    at_ctx(target),
                )
            )
        dest[me] = source[me]
        return copies

    def wait_all(copies):
        for copy in copies:
            copy.wait_recv()

    barrier = pltpu.get_barrier_semaphore()
    for step in range(1, nctx):
        pl.semaphore_signal(barrier, inc=1, device_id=at_ctx(peer(step)), device_id_type=MESH)
    for mate in (core_mate, side_mate):
        pl.semaphore_signal(barrier, inc=1, device_id=at_tp(mate), device_id_type=MESH)

    def pack_edges(picks, sources):
        total = None
        for index, source in enumerate(sources):
            block = merge_rows(source[...])
            term = lax.dot_general(
                picks[index], block, (((1,), (1,)), ((), ())), preferred_element_type=F32
            )
            total = term if total is None else total + term
        halo_out[...] = total.astype(BF16)

    def unpack_edges(picks):
        for index in range(3):
            spread = lax.dot_general(
                halo_in[...], picks[index], (((0,), (0,)), ((), ())), preferred_element_type=F32
            )
            edge[index] = spread.reshape(nctx, channels, width)

    loaded(0, 1, 2, 7)
    pack_edges(ends, (query, key, value))
    pl.semaphore_wait(barrier, nctx + 1)

    sent = []
    halo = send(halo_out, halo_in, halo_s.at[0], halo_r.at[0], at_ctx(peer(1)))
    loaded(6)
    own_rows = full_cot.at[pl.ds(mine * share, share)]
    to_side = send(cot, own_rows, cot_s.at[0], cot_r.at[0], at_tp(side_mate))
    to_core = send(cot, own_rows, cot_s.at[1], cot_r.at[1], at_tp(core_mate))
    sent += [to_side, to_core]
    full_cot[pl.ds(mine * share, share)] = cot[...]
    loaded(3)
    for index in range(3):
        padded = jnp.concatenate(
            [taps_in[index], jnp.zeros((taps.shape[3] - tap_count, nctx * channels), F32)], axis=0
        )
        taps[index] = padded.T.reshape(nctx, channels, taps.shape[3])

    def spectrum(spec):
        def one(k, carry):
            re = jnp.zeros((channels, width), F32)
            im = jnp.zeros((channels, width), F32)
            for n in range(nctx):
                block = signal[n]
                re = re + outer[0, k, n] * block
                im = im + outer[1, k, n] * block
            cos, sin = twists[0, k], twists[1, k]
            rows = pl.ds(pl.multiple_of(k * channels, channels), channels)
            work[rows, :width] = re * cos - im * sin
            work[rows, width:] = re * sin + im * cos
            return carry

        lax.fori_loop(0, kept, one, 0)
        spec[...] = dot_split(work[...], fwd_high[...], fwd_low[...])

    def inverse(re, im, store):
        work[:, :width] = re
        work[:, width:] = im
        work[...] = dot_split(work[...], bwd_high[...], bwd_low[...])

        def turn(k, carry):
            rows = pl.ds(pl.multiple_of(k * channels, channels), channels)
            back_re, back_im = work[rows, :width], work[rows, width:]
            cos, sin = twists[2, k], twists[3, k]
            parts[0, k] = back_re * cos + back_im * sin
            parts[1, k] = back_im * cos - back_re * sin
            return carry

        lax.fori_loop(0, kept, turn, 0)

        def one(n, carry):
            total = parts[0, 0]
            for k in range(1, kept):
                total = total + outer[0, k, n] * parts[0, k]
                if k < nctx:
                    total = total + outer[1, k, n] * parts[1, k]
            store(n, total)
            return carry

        lax.fori_loop(0, nctx, one, 0)

    lane = lax.broadcasted_iota(jnp.int32, (channels, width), 1)

    loaded(4, 9, 10, 11)
    for n in range(nctx):
        signal[n] = filters[:, n * width : (n + 1) * width]
    spectrum(spec_f)

    halo.wait()
    unpack_edges(ends)
    has_before = me > 0

    def short(index):
        source = (query, key, value)[index]

        def one(m, carry):
            tap = taps[index, m]
            here = source[m].astype(F32)
            before = jnp.where(has_before, edge[index, m], 0.0)
            total = tap[:, 0:1] * here
            for j in range(1, tap_count):
                moved = pltpu.roll(jnp.where(lane >= width - j, before, here), j, 1)
                total = total + tap[:, j : j + 1] * moved
            shorts[index, m] = total.astype(BF16)
            return carry

        lax.fori_loop(0, nctx, one, 0)

    short(1)
    short(2)
    product[...] = (shorts[1].astype(F32) * shorts[2].astype(F32)).astype(BF16)
    product_copies = exchange(product, product_chan, product_s, product_r)
    sent += product_copies
    short(0)

    to_side.wait_recv()
    passed_rows = full_cot.at[pl.ds(side_mate * share, share)]
    passed = send(passed_rows, passed_rows, cot_s.at[2], cot_r.at[2], at_tp(core_mate))
    sent.append(passed)
    loaded(5, 8, 12, 13)
    to_core.wait_recv()

    def gate_part(group):
        cot_block = full_cot[pl.ds(group * share, share)].reshape(block_rows, width)
        start = pl.multiple_of(group * block_rows, block_rows)
        return lax.dot_general(
            cot_block,
            weight[pl.ds(start, block_rows), :],
            (((0,), (0,)), ((), ())),
            preferred_element_type=F32,
        )

    total = gate_part(mine) + gate_part(core_mate) + gate_part(side_mate)
    passed.wait_recv()
    total = total + gate_part(far_mate)
    grad_gated[...] = total.T.reshape(nctx, channels, width)
    grad_conv[...] = (grad_gated[...] * shorts[0].astype(F32)).astype(BF16)
    grad_copies = exchange(grad_conv, grad_conv_chan, grad_s, grad_r)
    sent += grad_copies

    wait_all(product_copies)
    signal[...] = product_chan[...].astype(F32)
    spectrum(spec_p)

    f_re, f_im = spec_f[:, :width], spec_f[:, width:]
    p_re, p_im = spec_p[:, :width], spec_p[:, width:]

    def store_convolved(n, total):
        conv_chan[n] = total.astype(BF16)

    inverse(p_re * f_re - p_im * f_im, p_re * f_im + p_im * f_re, store_convolved)
    conv_copies = exchange(conv_chan, conv_here, conv_s, conv_r)
    sent += conv_copies

    row_copies = []
    for step in range(1, nctx):
        target = peer(step)
        row_copies.append(
            send(
                full_cot.at[target, mine],
                cot_rows.at[mine, me],
                rows_s.at[step],
                rows_r.at[step],
                at_ctx(target),
            )
        )
    sent += row_copies
    cot_rows[mine, me] = full_cot[me, mine]

    wait_all(grad_copies)
    signal[...] = grad_conv_chan[...].astype(F32)
    spectrum(spec_g)
    f_re, f_im = spec_f[:, :width], spec_f[:, width:]
    g_re, g_im = spec_g[:, :width], spec_g[:, width:]

    def store_product(n, total):
        grad_chan[n] = total.astype(BF16)

    inverse(f_re * g_re + f_im * g_im, f_re * g_im - f_im * g_re, store_product)
    back_copies = exchange(grad_chan, grad_here, back_s, back_r)
    sent += back_copies

    wait_all(conv_copies)
    gated_all[me] = (shorts[0].astype(F32) * conv_here[...].astype(F32)).astype(BF16)
    line = nctx // 2
    place = me // 2

    def relay(step, way, action):
        sign = 1 - 2 * way
        block = gated_all.at[me - sign * 2 * step]
        return pltpu.make_async_remote_copy(
            src_ref=block,
            dst_ref=block,
            send_sem=all_s.at[way, step],
            recv_sem=all_r.at[way, step + 1 - action],
            device_id=at_ctx(me + sign * (2 - 4 * action)),
            device_id_type=MESH,
        )

    def came(step, way):
        return place >= step if way == 0 else place < line - step

    def goes(step, way):
        more = place < line - 1 if way == 0 else place > 0
        return more if step == 0 else jnp.logical_and(came(step, way), more)

    def to_mate(spot):
        block = gated_all.at[2 * spot + me % 2]
        return pltpu.make_async_remote_copy(
            src_ref=block,
            dst_ref=block,
            send_sem=fwd_s.at[spot],
            recv_sem=fwd_r.at[spot],
            device_id=at_ctx(x_mate),
            device_id_type=MESH,
        )

    def pass_on(step):
        for way in range(2):
            if step:

                @pl.when(came(step, way))
                def _():
                    relay(step, way, 1).wait_recv()

            if step < line - 1:

                @pl.when(goes(step, way))
                def _():
                    relay(step, way, 0).start()

            if step:

                @pl.when(came(step, way))
                def _():
                    to_mate(place - step * (1 - 2 * way)).start()

        if step == 0:
            to_mate(place).start()

    pass_on(0)

    right = merge_rows(gated_all[me])

    def project(group):
        start = pl.multiple_of(group * block_rows, block_rows)
        return dot(weight[pl.ds(start, block_rows), :], right)

    core = mine % 2
    pair_copies = []
    for side in range(ntp // 2):
        partial[side] = project(2 * side + 1 - core).astype(BF16)
        pair_copies.append(
            send(
                partial.at[side],
                pair_in.at[side],
                pair_s.at[side],
                pair_r.at[side],
                at_tp(core_mate),
            )
        )
    sent += pair_copies

    wait_all(row_copies)
    own_quarter = cot_rows.at[mine]
    quarter_side = send(own_quarter, own_quarter, quart_s.at[0], quart_r.at[0], at_tp(side_mate))
    quarter_core = send(own_quarter, own_quarter, quart_s.at[1], quart_r.at[1], at_tp(core_mate))
    sent += [quarter_side, quarter_core]

    wait_all(back_copies)

    def gradients(m, carry):
        back = grad_here[m].astype(F32)
        shorts_grad[0, m] = (grad_gated[m] * conv_here[m].astype(F32)).astype(BF16)
        shorts_grad[1, m] = (back * shorts[2, m].astype(F32)).astype(BF16)
        shorts_grad[2, m] = (back * shorts[1, m].astype(F32)).astype(BF16)
        return carry

    lax.fori_loop(0, nctx, gradients, 0)
    pack_edges(starts, [shorts_grad.at[index] for index in range(3)])
    halo = send(halo_out, halo_in, halo_s.at[1], halo_r.at[1], at_ctx(peer(nctx - 1)))

    my_side = mine // 2
    wait_all(pair_copies)
    pair_sum[...] = (project(side_mate) + pair_in[1 - my_side].astype(F32)).astype(BF16)
    final = send(pair_sum, final_in, final_s, final_r, at_tp(side_mate))
    sent.append(final)

    pass_on(1)

    halo.wait()
    unpack_edges(starts)
    has_after = me < nctx - 1
    for index, result in enumerate((grad_query, grad_key, grad_value)):

        def long(m, carry, index=index, result=result):
            tap = taps[index, m]
            here = shorts_grad[index, m].astype(F32)
            after = jnp.where(has_after, edge[index, m], 0.0)
            total = tap[:, 0:1] * here
            for j in range(1, tap_count):
                moved = pltpu.roll(jnp.where(lane < j, after, here), width - j, 1)
                total = total + tap[:, j : j + 1] * moved
            result[m] = total.astype(BF16)
            return carry

        lax.fori_loop(0, nctx, long, 0)
        store(1 + index)

    for step in range(2, line - 1):
        pass_on(step)

    p_re, p_im = spec_p[:, :width], spec_p[:, width:]
    g_re, g_im = spec_g[:, :width], spec_g[:, width:]

    def store_filters(n, total):
        grad_filters[:, pl.ds(pl.multiple_of(n * width, width), width)] = total

    inverse(p_re * g_re + p_im * g_im, p_re * g_im - p_im * g_re, store_filters)
    store(4)
    if line > 2:
        pass_on(line - 1)
    quarter_side.wait_recv()
    far_quarter = cot_rows.at[side_mate]
    quarter_far = send(far_quarter, far_quarter, quart_s.at[2], quart_r.at[2], at_tp(core_mate))
    sent.append(quarter_far)

    own_sum = project(mine) + pair_in[my_side].astype(F32)
    final.wait_recv()
    mixed_out[...] = (own_sum + final_in[...].astype(F32)).astype(BF16)
    store(0)

    quarter_core.wait_recv()
    quarter_far.wait_recv()
    quarter = cot_rows.shape[2]

    def over_line(column):
        blocks = [merge_rows(gated_all[2 * spot + column]) for spot in range(line)]
        return jnp.concatenate(blocks, axis=1)

    def weigh(group, column, right):
        left = [cot_rows[group, 2 * spot + column] for spot in range(line)]
        return lax.dot_general(
            jnp.concatenate(left, axis=1),
            right,
            (((1,), (1,)), ((), ())),
            preferred_element_type=F32,
        )

    right = over_line(me % 2)
    for group in range(ntp):
        rows = slice(group * quarter, (group + 1) * quarter)
        grad_weight[rows, :] = weigh(group, me % 2, right)
    for spot in range(line):
        to_mate(spot).wait_recv()
    right = over_line(x_mate % 2)
    for group in range(ntp):
        rows = slice(group * quarter, (group + 1) * quarter)
        grad_weight[rows, :] += weigh(group, x_mate % 2, right)
        store(5, pl.ds(group * quarter, quarter), OUTPUTS - 1 + group)

    for copy in sent:
        copy.wait_send()
    for spot in range(line):
        to_mate(spot).wait_send()
    for step in range(line - 1):
        for way in range(2):

            @pl.when(goes(step, way))
            def _(step=step, way=way):
                relay(step, way, 0).wait_send()
    for copy in stores:
        copy.wait()


def hand_on(*refs):
    count = (len(refs) - 2) // 3
    sources, dests, held = refs[:count], refs[count : 2 * count], refs[2 * count : 3 * count]
    in_sem, out_sem = refs[3 * count :]
    loads = [
        pltpu.make_async_copy(source, place, in_sem.at[index])
        for index, (source, place) in enumerate(zip(sources, held))
    ]
    stores = [
        pltpu.make_async_copy(place, dest, out_sem.at[index])
        for index, (place, dest) in enumerate(zip(held, dests))
    ]
    for load in loads:
        load.start()
    for load, store in zip(loads, stores):
        load.wait()
        store.start()
    for store in stores:
        store.wait()


def per_device(nctx, ntp, query_in, key_in, value_in, short_weights, filters, out_weight, cotangent):
    rows, width = query_in.shape
    channels = rows // nctx
    features = out_weight.shape[0]
    quarter = features // (nctx * ntp)
    share = nctx // ntp
    kept = nctx + 1
    outer, twists, *inner = make_tables(nctx, width)
    tap_count = short_weights.shape[2]
    tap_slots = -(-tap_count // 8) * 8
    edge_rows = -(-3 * tap_slots // 16) * 16
    ends = np.zeros((3, edge_rows, width), np.float32)
    starts = np.zeros((3, edge_rows, width), np.float32)
    for index in range(3):
        for j in range(tap_count - 1):
            ends[index, index * tap_slots + j, width - (tap_count - 1) + j] = 1.0
            starts[index, index * tap_slots + j, j] = 1.0
    blocks = (nctx, channels, width)

    def bf(*shape):
        return pltpu.VMEM(shape, BF16)

    def f32(*shape):
        return pltpu.VMEM(shape, F32)

    def sems(*shape):
        return pltpu.SemaphoreType.DMA(shape)

    smem = pl.BlockSpec(memory_space=pltpu.SMEM)
    anywhere = pl.BlockSpec(memory_space=pl.ANY)
    out_shape = (
        jax.ShapeDtypeStruct((features // ntp, width), BF16),
        jax.ShapeDtypeStruct(blocks, BF16),
        jax.ShapeDtypeStruct(blocks, BF16),
        jax.ShapeDtypeStruct(blocks, BF16),
        jax.ShapeDtypeStruct((channels, nctx * width), F32),
        jax.ShapeDtypeStruct((features // nctx, rows), F32),
    )
    arrays = (
        query_in.reshape(blocks),
        key_in.reshape(blocks),
        value_in.reshape(blocks),
        short_weights.transpose(0, 2, 1),
        filters.reshape(channels, nctx * width),
        out_weight,
        cotangent.reshape(share, ntp, quarter, width),
        jnp.asarray(ends.astype(jnp.bfloat16)),
        jnp.asarray(starts.astype(jnp.bfloat16)),
        jnp.asarray(twists),
        *[jnp.asarray(table) for table in inner],
    )
    outs = pl.pallas_call(
        functools.partial(kernel, nctx, ntp),
        out_shape=out_shape,
        in_specs=[smem] + [anywhere] * INPUTS,
        out_specs=tuple([anywhere] * OUTPUTS),
        scratch_shapes=[pltpu.VMEM(array.shape, array.dtype) for array in arrays]
        + [pltpu.VMEM(shape.shape, shape.dtype) for shape in out_shape]
        + [
            sems(INPUTS),
            sems(OUTPUTS - 1 + ntp),
            bf(nctx, ntp, quarter, width),
            bf(ntp, nctx, quarter, width),
            f32(3, nctx, channels, tap_slots),
            bf(edge_rows, rows),
            bf(edge_rows, rows),
            f32(3, *blocks),
            bf(3, *blocks),
            f32(*blocks),
            f32(kept * channels, 2 * width),
            f32(2, kept, channels, width),
            f32(kept * channels, 2 * width),
            f32(kept * channels, 2 * width),
            f32(kept * channels, 2 * width),
            bf(*blocks),
            bf(*blocks),
            bf(*blocks),
            bf(*blocks),
            bf(nctx, *blocks),
            f32(*blocks),
            bf(*blocks),
            bf(*blocks),
            bf(*blocks),
            bf(*blocks),
            bf(3, *blocks),
            bf(ntp // 2, features // ntp, width),
            bf(ntp // 2, features // ntp, width),
            bf(features // ntp, width),
            bf(features // ntp, width),
            sems(2),
            sems(2),
            sems(3),
            sems(3),
            sems(nctx),
            sems(nctx),
            sems(3),
            sems(3),
            sems(nctx),
            sems(nctx),
            sems(nctx),
            sems(nctx),
            sems(nctx),
            sems(nctx),
            sems(nctx),
            sems(nctx),
            sems(2, nctx // 2),
            sems(2, nctx // 2),
            sems(nctx),
            sems(nctx),
            sems(ntp // 2),
            sems(ntp // 2),
            pltpu.SemaphoreType.DMA,
            pltpu.SemaphoreType.DMA,
        ],
        compiler_params=pltpu.CompilerParams(
            collective_id=0, has_side_effects=True, vmem_limit_bytes=56 * 1024 * 1024
        ),
        cost_estimate=pl.CostEstimate(
            flops=6 * features * rows * width, bytes_accessed=10 * features * rows // 4, transcendentals=0
        ),
        name="mixer",
    )(
        jnp.asarray(outer),
        *arrays,
    )
    outs = pl.pallas_call(
        hand_on,
        out_shape=out_shape,
        in_specs=[anywhere] * OUTPUTS,
        out_specs=tuple([anywhere] * OUTPUTS),
        scratch_shapes=[pltpu.VMEM(shape.shape, shape.dtype) for shape in out_shape]
        + [sems(OUTPUTS), sems(OUTPUTS)],
        compiler_params=pltpu.CompilerParams(vmem_limit_bytes=56 * 1024 * 1024),
        name="hand_on",
    )(*outs)
    mixed, grad_query, grad_key, grad_value, grad_filters, grad_weight = outs
    return (
        mixed,
        grad_query.reshape(rows, width),
        grad_key.reshape(rows, width),
        grad_value.reshape(rows, width),
        grad_filters.reshape(filters.shape),
        grad_weight,
    )


def solution(mesh):
    placed = (
        P("tp", "ctx"),
        P("tp", "ctx"),
        P("tp", "ctx"),
        P(None, "tp", None),
        P("tp", "ctx", None),
        P(None, "tp"),
        P("tp", "ctx"),
    )
    return jax.shard_map(
        functools.partial(per_device, mesh.shape["ctx"], mesh.shape["tp"]),
        mesh=mesh,
        in_specs=placed,
        out_specs=(
            P("tp", "ctx"),
            P("tp", "ctx"),
            P("tp", "ctx"),
            P("tp", "ctx"),
            P("tp", "ctx", None),
            P("ctx", "tp"),
        ),
        check_vma=False,
    )
```

```python
import functools

import jax
import jax.numpy as jnp
import numpy as np
from jax import lax
from jax.experimental import pallas as pl
from jax.experimental.pallas import tpu as pltpu
from jax.sharding import PartitionSpec as P

F32 = jnp.float32
BF16 = jnp.bfloat16
MESH = pl.DeviceIdType.MESH


def split_table(table):
    table = table.astype(np.float32)
    high = table.astype(jnp.bfloat16)
    low = (table - high.astype(np.float32)).astype(jnp.bfloat16)
    return high, low


def make_tables(blocks, width):
    rows = 2 * blocks
    full = rows * width
    kept = blocks + 1
    turn = np.outer(np.arange(kept), np.arange(blocks)) % rows * (2 * np.pi / rows)
    outer = np.stack([np.cos(turn), -np.sin(turn)]).astype(np.float32)
    twist = np.outer(np.arange(kept), np.arange(width)) % full * (2 * np.pi / full)
    weight = np.full((kept, 1), 2.0 / full)
    weight[0] = weight[-1] = 1.0 / full
    twists = np.stack(
        [np.cos(twist), -np.sin(twist), weight * np.cos(twist), weight * -np.sin(twist)]
    ).astype(np.float32)[:, :, None, :]
    inner = np.outer(np.arange(width), np.arange(width)) % width * (2 * np.pi / width)
    re, im = np.cos(inner), -np.sin(inner)
    forward = np.block([[re, im], [-im, re]])
    backward = np.block([[re, -im], [im, re]])
    return outer, twists, *split_table(forward), *split_table(backward)


def dot(a, b):
    return jnp.dot(a, b, preferred_element_type=F32)


def dot_split(value, high, low):
    value_high = value.astype(BF16)
    value_low = (value - value_high.astype(F32)).astype(BF16)
    return dot(value_high, high) + dot(value_low, high) + dot(value_high, low)


def merge_rows(value):
    blocks, rows, lanes = value.shape
    if rows % 16:
        return value.astype(F32).reshape(blocks * rows, lanes).astype(BF16)
    return value.reshape(blocks * rows, lanes)


INPUTS = 14
OUTPUTS = 6


def kernel(nctx, ntp, outer, *refs):
    given, refs = refs[:INPUTS], refs[INPUTS:]
    wanted, refs = refs[:OUTPUTS], refs[OUTPUTS:]
    held, refs = refs[:INPUTS], refs[INPUTS:]
    made, refs = refs[:OUTPUTS], refs[OUTPUTS:]
    in_sem, out_sem, *refs = refs
    loads = {}
    for index in (0, 1, 2, 7, 6, 3, 4, 9, 10, 11, 12, 13, 8, 5):
        loads[index] = pltpu.make_async_copy(given[index], held[index], in_sem.at[index])
        loads[index].start()

    def loaded(*indices):
        for index in indices:
            loads[index].wait()

    stores = []

    def store(index, rows=None, slot=None):
        source, dest = made[index], wanted[index]
        if rows is not None:
            source, dest = source.at[rows], dest.at[rows]
        copy = pltpu.make_async_copy(source, dest, out_sem.at[index if slot is None else slot])
        copy.start()
        stores.append(copy)

    (
        query,
        key,
        value,
        taps_in,
        filters,
        weight,
        cot,
        ends,
        starts,
        twists,
        fwd_high,
        fwd_low,
        bwd_high,
        bwd_low,
    ) = held
    (
        mixed_out,
        grad_query,
        grad_key,
        grad_value,
        grad_filters,
        grad_weight,
    ) = made
    (
        full_cot,
        cot_rows,
        taps,
        halo_out,
        halo_in,
        edge,
        shorts,
        signal,
        work,
        parts,
        spec_f,
        spec_p,
        spec_g,
        product,
        product_chan,
        conv_chan,
        conv_here,
        gated_all,
        grad_gated,
        grad_conv,
        grad_conv_chan,
        grad_chan,
        grad_here,
        shorts_grad,
        partial,
        pair_in,
        pair_sum,
        final_in,
        halo_s,
        halo_r,
        cot_s,
        cot_r,
        rows_s,
        rows_r,
        quart_s,
        quart_r,
        product_s,
        product_r,
        conv_s,
        conv_r,
        grad_s,
        grad_r,
        back_s,
        back_r,
        all_s,
        all_r,
        fwd_s,
        fwd_r,
        pair_s,
        pair_r,
        final_s,
        final_r,
    ) = refs
    channels, width = query.shape[1:]
    kept = nctx + 1
    tap_count = taps_in.shape[1]
    me = lax.axis_index("ctx")
    mine = lax.axis_index("tp")
    core_mate = mine + 1 - 2 * (mine % 2)
    side_mate = (mine + ntp // 2) % ntp
    far_mate = (core_mate + ntp // 2) % ntp
    x_mate = me + 1 - 2 * (me % 2)
    share = nctx // ntp
    block_rows = cot.shape[0] * cot.shape[1] * cot.shape[2]

    def send(src, dst, send_sem, recv_sem, device):
        copy = pltpu.make_async_remote_copy(
            src_ref=src,
            dst_ref=dst,
            send_sem=send_sem,
            recv_sem=recv_sem,
            device_id=device,
            device_id_type=MESH,
        )
        copy.start()
        return copy

    def peer(step):
        return lax.rem(me + step, nctx)

    def at_ctx(target):
        return (target, mine)

    def at_tp(target):
        return (me, target)

    def exchange(source, dest, send_sem, recv_sem):
        copies = []
        for step in range(1, nctx):
            target = peer(step)
            copies.append(
                send(
                    source.at[target],
                    dest.at[me],
                    send_sem.at[step],
                    recv_sem.at[step],
                    at_ctx(target),
                )
            )
        dest[me] = source[me]
        return copies

    def wait_all(copies):
        for copy in copies:
            copy.wait_recv()

    barrier = pltpu.get_barrier_semaphore()
    for step in range(1, nctx):
        pl.semaphore_signal(barrier, inc=1, device_id=at_ctx(peer(step)), device_id_type=MESH)
    for mate in (core_mate, side_mate):
        pl.semaphore_signal(barrier, inc=1, device_id=at_tp(mate), device_id_type=MESH)

    def pack_edges(picks, sources):
        total = None
        for index, source in enumerate(sources):
            block = merge_rows(source[...])
            term = lax.dot_general(
                picks[index], block, (((1,), (1,)), ((), ())), preferred_element_type=F32
            )
            total = term if total is None else total + term
        halo_out[...] = total.astype(BF16)

    def unpack_edges(picks):
        for index in range(3):
            spread = lax.dot_general(
                halo_in[...], picks[index], (((0,), (0,)), ((), ())), preferred_element_type=F32
            )
            edge[index] = spread.reshape(nctx, channels, width)

    loaded(0, 1, 2, 7)
    pack_edges(ends, (query, key, value))
    pl.semaphore_wait(barrier, nctx + 1)

    sent = []
    halo = send(halo_out, halo_in, halo_s.at[0], halo_r.at[0], at_ctx(peer(1)))
    loaded(6)
    own_rows = full_cot.at[pl.ds(mine * share, share)]
    to_side = send(cot, own_rows, cot_s.at[0], cot_r.at[0], at_tp(side_mate))
    to_core = send(cot, own_rows, cot_s.at[1], cot_r.at[1], at_tp(core_mate))
    sent += [to_side, to_core]
    full_cot[pl.ds(mine * share, share)] = cot[...]
    loaded(3)
    for index in range(3):
        padded = jnp.concatenate(
            [taps_in[index], jnp.zeros((taps.shape[3] - tap_count, nctx * channels), F32)], axis=0
        )
        taps[index] = padded.T.reshape(nctx, channels, taps.shape[3])

    def spectrum(spec):
        def one(k, carry):
            re = jnp.zeros((channels, width), F32)
            im = jnp.zeros((channels, width), F32)
            for n in range(nctx):
                block = signal[n]
                re = re + outer[0, k, n] * block
                im = im + outer[1, k, n] * block
            cos, sin = twists[0, k], twists[1, k]
            rows = pl.ds(pl.multiple_of(k * channels, channels), channels)
            work[rows, :width] = re * cos - im * sin
            work[rows, width:] = re * sin + im * cos
            return carry

        lax.fori_loop(0, kept, one, 0)
        spec[...] = dot_split(work[...], fwd_high[...], fwd_low[...])

    def inverse(re, im, store):
        work[:, :width] = re
        work[:, width:] = im
        work[...] = dot_split(work[...], bwd_high[...], bwd_low[...])

        def turn(k, carry):
            rows = pl.ds(pl.multiple_of(k * channels, channels), channels)
            back_re, back_im = work[rows, :width], work[rows, width:]
            cos, sin = twists[2, k], twists[3, k]
            parts[0, k] = back_re * cos + back_im * sin
            parts[1, k] = back_im * cos - back_re * sin
            return carry

        lax.fori_loop(0, kept, turn, 0)

        def one(n, carry):
            total = parts[0, 0]
            for k in range(1, kept):
                total = total + outer[0, k, n] * parts[0, k]
                if k < nctx:
                    total = total + outer[1, k, n] * parts[1, k]
            store(n, total)
            return carry

        lax.fori_loop(0, nctx, one, 0)

    lane = lax.broadcasted_iota(jnp.int32, (channels, width), 1)

    loaded(4, 9, 10, 11)
    for n in range(nctx):
        signal[n] = filters[:, n * width : (n + 1) * width]
    spectrum(spec_f)

    halo.wait()
    unpack_edges(ends)
    has_before = me > 0

    def short(index):
        source = (query, key, value)[index]

        def one(m, carry):
            tap = taps[index, m]
            here = source[m].astype(F32)
            before = jnp.where(has_before, edge[index, m], 0.0)
            total = tap[:, 0:1] * here
            for j in range(1, tap_count):
                moved = pltpu.roll(jnp.where(lane >= width - j, before, here), j, 1)
                total = total + tap[:, j : j + 1] * moved
            shorts[index, m] = total.astype(BF16)
            return carry

        lax.fori_loop(0, nctx, one, 0)

    short(1)
    short(2)
    product[...] = (shorts[1].astype(F32) * shorts[2].astype(F32)).astype(BF16)
    product_copies = exchange(product, product_chan, product_s, product_r)
    sent += product_copies
    row_copies = [
        pltpu.make_async_remote_copy(
            src_ref=full_cot.at[peer(step), mine],
            dst_ref=cot_rows.at[mine, me],
            send_sem=rows_s.at[step],
            recv_sem=rows_r.at[step],
            device_id=at_ctx(peer(step)),
            device_id_type=MESH,
        )
        for step in range(1, nctx)
    ]
    sent += row_copies

    def send_rows(held_first):
        for step, copy in zip(range(1, nctx), row_copies):
            first = (peer(step) // share) // 2 == mine // 2

            @pl.when(first if held_first else jnp.logical_not(first))
            def _(copy=copy):
                copy.start()

    to_core.wait_recv()
    send_rows(True)
    short(0)

    to_side.wait_recv()
    passed_rows = full_cot.at[pl.ds(side_mate * share, share)]
    passed = send(passed_rows, passed_rows, cot_s.at[2], cot_r.at[2], at_tp(core_mate))
    sent.append(passed)

    wait_all(product_copies)
    loaded(5, 8, 12, 13)
    signal[...] = product_chan[...].astype(F32)
    spectrum(spec_p)
    passed.wait_recv()
    send_rows(False)
    cot_rows[mine, me] = full_cot[me, mine]

    f_re, f_im = spec_f[:, :width], spec_f[:, width:]
    p_re, p_im = spec_p[:, :width], spec_p[:, width:]

    def store_convolved(n, total):
        conv_chan[n] = total.astype(BF16)

    inverse(p_re * f_re - p_im * f_im, p_re * f_im + p_im * f_re, store_convolved)
    conv_copies = exchange(conv_chan, conv_here, conv_s, conv_r)
    sent += conv_copies


    def gate_part(group):
        cot_block = full_cot[pl.ds(group * share, share)].reshape(block_rows, width)
        start = pl.multiple_of(group * block_rows, block_rows)
        return lax.dot_general(
            cot_block,
            weight[pl.ds(start, block_rows), :],
            (((0,), (0,)), ((), ())),
            preferred_element_type=F32,
        )

    total = gate_part(mine) + gate_part(core_mate) + gate_part(side_mate)
    total = total + gate_part(far_mate)
    grad_gated[...] = total.T.reshape(nctx, channels, width)
    grad_conv[...] = (grad_gated[...] * shorts[0].astype(F32)).astype(BF16)
    grad_copies = exchange(grad_conv, grad_conv_chan, grad_s, grad_r)
    sent += grad_copies

    wait_all(conv_copies)
    gated_all[me] = (shorts[0].astype(F32) * conv_here[...].astype(F32)).astype(BF16)
    line = nctx // 2
    place = me // 2

    def relay(step, way, action):
        sign = 1 - 2 * way
        block = gated_all.at[me - sign * 2 * step]
        return pltpu.make_async_remote_copy(
            src_ref=block,
            dst_ref=block,
            send_sem=all_s.at[way, step],
            recv_sem=all_r.at[way, step + 1 - action],
            device_id=at_ctx(me + sign * (2 - 4 * action)),
            device_id_type=MESH,
        )

    def came(step, way):
        return place >= step if way == 0 else place < line - step

    def goes(step, way):
        more = place < line - 1 if way == 0 else place > 0
        return more if step == 0 else jnp.logical_and(came(step, way), more)

    def to_mate(spot):
        block = gated_all.at[2 * spot + me % 2]
        return pltpu.make_async_remote_copy(
            src_ref=block,
            dst_ref=block,
            send_sem=fwd_s.at[spot],
            recv_sem=fwd_r.at[spot],
            device_id=at_ctx(x_mate),
            device_id_type=MESH,
        )

    def pass_on(step):
        for way in range(2):
            if step:

                @pl.when(came(step, way))
                def _():
                    relay(step, way, 1).wait_recv()

            if step < line - 1:

                @pl.when(goes(step, way))
                def _():
                    relay(step, way, 0).start()

            if step:

                @pl.when(came(step, way))
                def _():
                    to_mate(place - step * (1 - 2 * way)).start()

        if step == 0:
            to_mate(place).start()

    pass_on(0)

    right = merge_rows(gated_all[me])

    def project(group):
        start = pl.multiple_of(group * block_rows, block_rows)
        return dot(weight[pl.ds(start, block_rows), :], right)

    core = mine % 2
    pair_copies = []
    for side in range(ntp // 2):
        partial[side] = project(2 * side + 1 - core).astype(BF16)
        pair_copies.append(
            send(
                partial.at[side],
                pair_in.at[side],
                pair_s.at[side],
                pair_r.at[side],
                at_tp(core_mate),
            )
        )
    sent += pair_copies

    wait_all(row_copies)
    own_quarter = cot_rows.at[mine]
    quarter_side = send(own_quarter, own_quarter, quart_s.at[0], quart_r.at[0], at_tp(side_mate))
    quarter_core = send(own_quarter, own_quarter, quart_s.at[1], quart_r.at[1], at_tp(core_mate))
    sent += [quarter_side, quarter_core]

    wait_all(grad_copies)
    signal[...] = grad_conv_chan[...].astype(F32)
    spectrum(spec_g)
    f_re, f_im = spec_f[:, :width], spec_f[:, width:]
    g_re, g_im = spec_g[:, :width], spec_g[:, width:]

    def store_product(n, total):
        grad_chan[n] = total.astype(BF16)

    inverse(f_re * g_re + f_im * g_im, f_re * g_im - f_im * g_re, store_product)
    back_copies = exchange(grad_chan, grad_here, back_s, back_r)
    sent += back_copies

    pass_on(1)

    my_side = mine // 2
    wait_all(pair_copies)
    pair_sum[...] = (project(side_mate) + pair_in[1 - my_side].astype(F32)).astype(BF16)
    final = send(pair_sum, final_in, final_s, final_r, at_tp(side_mate))
    sent.append(final)

    wait_all(back_copies)

    def gradients(m, carry):
        back = grad_here[m].astype(F32)
        shorts_grad[0, m] = (grad_gated[m] * conv_here[m].astype(F32)).astype(BF16)
        shorts_grad[1, m] = (back * shorts[2, m].astype(F32)).astype(BF16)
        shorts_grad[2, m] = (back * shorts[1, m].astype(F32)).astype(BF16)
        return carry

    lax.fori_loop(0, nctx, gradients, 0)
    pack_edges(starts, [shorts_grad.at[index] for index in range(3)])
    halo = send(halo_out, halo_in, halo_s.at[1], halo_r.at[1], at_ctx(peer(nctx - 1)))

    for step in range(2, line - 1):
        pass_on(step)

    p_re, p_im = spec_p[:, :width], spec_p[:, width:]
    g_re, g_im = spec_g[:, :width], spec_g[:, width:]

    def store_filters(n, total):
        grad_filters[:, pl.ds(pl.multiple_of(n * width, width), width)] = total

    inverse(p_re * g_re + p_im * g_im, p_re * g_im - p_im * g_re, store_filters)
    store(4)
    halo.wait()
    unpack_edges(starts)
    has_after = me < nctx - 1
    for index, result in enumerate((grad_query, grad_key, grad_value)):

        def long(m, carry, index=index, result=result):
            tap = taps[index, m]
            here = shorts_grad[index, m].astype(F32)
            after = jnp.where(has_after, edge[index, m], 0.0)
            total = tap[:, 0:1] * here
            for j in range(1, tap_count):
                moved = pltpu.roll(jnp.where(lane < j, after, here), width - j, 1)
                total = total + tap[:, j : j + 1] * moved
            result[m] = total.astype(BF16)
            return carry

        lax.fori_loop(0, nctx, long, 0)
        store(1 + index)

    if line > 2:
        pass_on(line - 1)
    quarter_side.wait_recv()
    far_quarter = cot_rows.at[side_mate]
    quarter_far = send(far_quarter, far_quarter, quart_s.at[2], quart_r.at[2], at_tp(core_mate))
    sent.append(quarter_far)

    own_sum = project(mine) + pair_in[my_side].astype(F32)
    final.wait_recv()
    mixed_out[...] = (own_sum + final_in[...].astype(F32)).astype(BF16)
    store(0)

    quarter_core.wait_recv()
    quarter_far.wait_recv()
    quarter = cot_rows.shape[2]

    def over_line(column):
        blocks = [merge_rows(gated_all[2 * spot + column]) for spot in range(line)]
        return jnp.concatenate(blocks, axis=1)

    def weigh(group, column, right):
        left = [cot_rows[group, 2 * spot + column] for spot in range(line)]
        return lax.dot_general(
            jnp.concatenate(left, axis=1),
            right,
            (((1,), (1,)), ((), ())),
            preferred_element_type=F32,
        )

    right = over_line(me % 2)
    for group in range(ntp):
        rows = slice(group * quarter, (group + 1) * quarter)
        grad_weight[rows, :] = weigh(group, me % 2, right)
    for spot in range(line):
        to_mate(spot).wait_recv()
    right = over_line(x_mate % 2)
    for group in range(ntp):
        rows = slice(group * quarter, (group + 1) * quarter)
        grad_weight[rows, :] += weigh(group, x_mate % 2, right)
        store(5, pl.ds(group * quarter, quarter), OUTPUTS - 1 + group)

    for copy in sent:
        copy.wait_send()
    for spot in range(line):
        to_mate(spot).wait_send()
    for step in range(line - 1):
        for way in range(2):

            @pl.when(goes(step, way))
            def _(step=step, way=way):
                relay(step, way, 0).wait_send()
    for copy in stores:
        copy.wait()


def hand_on(*refs):
    count = (len(refs) - 2) // 3
    sources, dests, held = refs[:count], refs[count : 2 * count], refs[2 * count : 3 * count]
    in_sem, out_sem = refs[3 * count :]
    loads = [
        pltpu.make_async_copy(source, place, in_sem.at[index])
        for index, (source, place) in enumerate(zip(sources, held))
    ]
    stores = [
        pltpu.make_async_copy(place, dest, out_sem.at[index])
        for index, (place, dest) in enumerate(zip(held, dests))
    ]
    for load in loads:
        load.start()
    for load, store in zip(loads, stores):
        load.wait()
        store.start()
    for store in stores:
        store.wait()


def per_device(nctx, ntp, query_in, key_in, value_in, short_weights, filters, out_weight, cotangent):
    rows, width = query_in.shape
    channels = rows // nctx
    features = out_weight.shape[0]
    quarter = features // (nctx * ntp)
    share = nctx // ntp
    kept = nctx + 1
    outer, twists, *inner = make_tables(nctx, width)
    tap_count = short_weights.shape[2]
    tap_slots = -(-tap_count // 8) * 8
    edge_rows = -(-3 * tap_slots // 16) * 16
    ends = np.zeros((3, edge_rows, width), np.float32)
    starts = np.zeros((3, edge_rows, width), np.float32)
    for index in range(3):
        for j in range(tap_count - 1):
            ends[index, index * tap_slots + j, width - (tap_count - 1) + j] = 1.0
            starts[index, index * tap_slots + j, j] = 1.0
    blocks = (nctx, channels, width)

    def bf(*shape):
        return pltpu.VMEM(shape, BF16)

    def f32(*shape):
        return pltpu.VMEM(shape, F32)

    def sems(*shape):
        return pltpu.SemaphoreType.DMA(shape)

    smem = pl.BlockSpec(memory_space=pltpu.SMEM)
    anywhere = pl.BlockSpec(memory_space=pl.ANY)
    out_shape = (
        jax.ShapeDtypeStruct((features // ntp, width), BF16),
        jax.ShapeDtypeStruct(blocks, BF16),
        jax.ShapeDtypeStruct(blocks, BF16),
        jax.ShapeDtypeStruct(blocks, BF16),
        jax.ShapeDtypeStruct((channels, nctx * width), F32),
        jax.ShapeDtypeStruct((features // nctx, rows), F32),
    )
    arrays = (
        query_in.reshape(blocks),
        key_in.reshape(blocks),
        value_in.reshape(blocks),
        short_weights.transpose(0, 2, 1),
        filters.reshape(channels, nctx * width),
        out_weight,
        cotangent.reshape(share, ntp, quarter, width),
        jnp.asarray(ends.astype(jnp.bfloat16)),
        jnp.asarray(starts.astype(jnp.bfloat16)),
        jnp.asarray(twists),
        *[jnp.asarray(table) for table in inner],
    )
    outs = pl.pallas_call(
        functools.partial(kernel, nctx, ntp),
        out_shape=out_shape,
        in_specs=[smem] + [anywhere] * INPUTS,
        out_specs=tuple([anywhere] * OUTPUTS),
        scratch_shapes=[pltpu.VMEM(array.shape, array.dtype) for array in arrays]
        + [pltpu.VMEM(shape.shape, shape.dtype) for shape in out_shape]
        + [
            sems(INPUTS),
            sems(OUTPUTS - 1 + ntp),
            bf(nctx, ntp, quarter, width),
            bf(ntp, nctx, quarter, width),
            f32(3, nctx, channels, tap_slots),
            bf(edge_rows, rows),
            bf(edge_rows, rows),
            f32(3, *blocks),
            bf(3, *blocks),
            f32(*blocks),
            f32(kept * channels, 2 * width),
            f32(2, kept, channels, width),
            f32(kept * channels, 2 * width),
            f32(kept * channels, 2 * width),
            f32(kept * channels, 2 * width),
            bf(*blocks),
            bf(*blocks),
            bf(*blocks),
            bf(*blocks),
            bf(nctx, *blocks),
            f32(*blocks),
            bf(*blocks),
            bf(*blocks),
            bf(*blocks),
            bf(*blocks),
            bf(3, *blocks),
            bf(ntp // 2, features // ntp, width),
            bf(ntp // 2, features // ntp, width),
            bf(features // ntp, width),
            bf(features // ntp, width),
            sems(2),
            sems(2),
            sems(3),
            sems(3),
            sems(nctx),
            sems(nctx),
            sems(3),
            sems(3),
            sems(nctx),
            sems(nctx),
            sems(nctx),
            sems(nctx),
            sems(nctx),
            sems(nctx),
            sems(nctx),
            sems(nctx),
            sems(2, nctx // 2),
            sems(2, nctx // 2),
            sems(nctx),
            sems(nctx),
            sems(ntp // 2),
            sems(ntp // 2),
            pltpu.SemaphoreType.DMA,
            pltpu.SemaphoreType.DMA,
        ],
        compiler_params=pltpu.CompilerParams(
            collective_id=0, has_side_effects=True, vmem_limit_bytes=56 * 1024 * 1024
        ),
        cost_estimate=pl.CostEstimate(
            flops=6 * features * rows * width, bytes_accessed=10 * features * rows // 4, transcendentals=0
        ),
        name="mixer",
    )(
        jnp.asarray(outer),
        *arrays,
    )
    outs = pl.pallas_call(
        hand_on,
        out_shape=out_shape,
        in_specs=[anywhere] * OUTPUTS,
        out_specs=tuple([anywhere] * OUTPUTS),
        scratch_shapes=[pltpu.VMEM(shape.shape, shape.dtype) for shape in out_shape]
        + [sems(OUTPUTS), sems(OUTPUTS)],
        compiler_params=pltpu.CompilerParams(vmem_limit_bytes=56 * 1024 * 1024),
        name="hand_on",
    )(*outs)
    mixed, grad_query, grad_key, grad_value, grad_filters, grad_weight = outs
    return (
        mixed,
        grad_query.reshape(rows, width),
        grad_key.reshape(rows, width),
        grad_value.reshape(rows, width),
        grad_filters.reshape(filters.shape),
        grad_weight,
    )


def solution(mesh):
    placed = (
        P("tp", "ctx"),
        P("tp", "ctx"),
        P("tp", "ctx"),
        P(None, "tp", None),
        P("tp", "ctx", None),
        P(None, "tp"),
        P("tp", "ctx"),
    )
    return jax.shard_map(
        functools.partial(per_device, mesh.shape["ctx"], mesh.shape["tp"]),
        mesh=mesh,
        in_specs=placed,
        out_specs=(
            P("tp", "ctx"),
            P("tp", "ctx"),
            P("tp", "ctx"),
            P("tp", "ctx"),
            P("tp", "ctx", None),
            P("ctx", "tp"),
        ),
        check_vma=False,
    )
```

```python
import functools

import jax
import jax.numpy as jnp
import numpy as np
from jax import lax
from jax.experimental import pallas as pl
from jax.experimental.pallas import tpu as pltpu
from jax.sharding import PartitionSpec as P

F32 = jnp.float32
BF16 = jnp.bfloat16
MESH = pl.DeviceIdType.MESH


def split_table(table):
    table = table.astype(np.float32)
    high = table.astype(jnp.bfloat16)
    low = (table - high.astype(np.float32)).astype(jnp.bfloat16)
    return high, low


def make_tables(blocks, width):
    rows = 2 * blocks
    full = rows * width
    kept = blocks + 1
    turn = np.outer(np.arange(kept), np.arange(blocks)) % rows * (2 * np.pi / rows)
    outer = np.stack([np.cos(turn), -np.sin(turn)])
    twist = np.outer(np.arange(kept), np.arange(width)) % full * (2 * np.pi / full)
    weight = np.full((kept, 1), 2.0 / full)
    weight[0] = weight[-1] = 1.0 / full
    twists = np.stack(
        [np.cos(twist), -np.sin(twist), weight * np.cos(twist), weight * -np.sin(twist)]
    ).astype(np.float32)[:, :, None, :]
    inner = np.outer(np.arange(width), np.arange(width)) % width * (2 * np.pi / width)
    re, im = np.cos(inner), -np.sin(inner)
    forward = np.block([[re, im], [-im, re]])
    backward = np.block([[re, -im], [im, re]])
    return outer, twists, *split_table(forward), *split_table(backward)


def dot(a, b):
    return jnp.dot(a, b, preferred_element_type=F32)


def dot_split(value, high, low):
    value_high = value.astype(BF16)
    value_low = (value - value_high.astype(F32)).astype(BF16)
    return dot(value_high, high) + dot(value_low, high) + dot(value_high, low)


def repeat(count, body):
    if count <= 16:
        for index in range(count):
            body(index, 0)
    else:
        lax.fori_loop(0, count, body, 0)


def window(index, size):
    if isinstance(index, int):
        return pl.ds(index * size, size)
    return pl.ds(pl.multiple_of(index * size, size), size)


def add_term(total, factor, block):
    if isinstance(factor, float):
        if abs(factor) < 1e-9:
            return total
        if abs(abs(factor) - 1.0) < 1e-9:
            if total is None:
                return block if factor > 0 else -block
            return total + block if factor > 0 else total - block
    term = factor * block
    return term if total is None else total + term


def merge_rows(value):
    blocks, rows, lanes = value.shape
    if rows % 16:
        return value.astype(F32).reshape(blocks * rows, lanes).astype(BF16)
    return value.reshape(blocks * rows, lanes)


INPUTS = 14
OUTPUTS = 6


def kernel(nctx, ntp, outer, *refs):
    given, refs = refs[:INPUTS], refs[INPUTS:]
    wanted, refs = refs[:OUTPUTS], refs[OUTPUTS:]
    held, refs = refs[:INPUTS], refs[INPUTS:]
    made, refs = refs[:OUTPUTS], refs[OUTPUTS:]
    in_sem, out_sem, *refs = refs
    loads = {}
    for index in (0, 1, 2, 7, 6, 3, 4, 9, 10, 11, 12, 13, 8, 5):
        loads[index] = pltpu.make_async_copy(given[index], held[index], in_sem.at[index])
        loads[index].start()

    def loaded(*indices):
        for index in indices:
            loads[index].wait()

    stores = []

    def store(index, rows=None, slot=None):
        source, dest = made[index], wanted[index]
        if rows is not None:
            source, dest = source.at[rows], dest.at[rows]
        copy = pltpu.make_async_copy(source, dest, out_sem.at[index if slot is None else slot])
        copy.start()
        stores.append(copy)

    (
        query,
        key,
        value,
        taps_in,
        filters,
        weight,
        cot,
        ends,
        starts,
        twists,
        fwd_high,
        fwd_low,
        bwd_high,
        bwd_low,
    ) = held
    (
        mixed_out,
        grad_query,
        grad_key,
        grad_value,
        grad_filters,
        grad_weight,
    ) = made
    (
        full_cot,
        cot_rows,
        taps,
        halo_out,
        halo_in,
        edge,
        shorts,
        signal,
        work,
        parts,
        spec_f,
        spec_p,
        spec_g,
        product,
        product_chan,
        conv_chan,
        conv_here,
        gated_all,
        grad_gated,
        grad_conv,
        grad_conv_chan,
        grad_chan,
        grad_here,
        shorts_grad,
        partial,
        pair_in,
        pair_sum,
        final_in,
        halo_s,
        halo_r,
        cot_s,
        cot_r,
        rows_s,
        rows_r,
        quart_s,
        quart_r,
        product_s,
        product_r,
        conv_s,
        conv_r,
        grad_s,
        grad_r,
        back_s,
        back_r,
        all_s,
        all_r,
        fwd_s,
        fwd_r,
        pair_s,
        pair_r,
        final_s,
        final_r,
    ) = refs
    channels, width = query.shape[1:]
    kept = nctx + 1
    tap_count = taps_in.shape[1]
    me = lax.axis_index("ctx")
    mine = lax.axis_index("tp")
    core_mate = mine + 1 - 2 * (mine % 2)
    side_mate = (mine + ntp // 2) % ntp
    far_mate = (core_mate + ntp // 2) % ntp
    x_mate = me + 1 - 2 * (me % 2)
    share = nctx // ntp
    block_rows = cot.shape[0] * cot.shape[1] * cot.shape[2]

    def send(src, dst, send_sem, recv_sem, device):
        copy = pltpu.make_async_remote_copy(
            src_ref=src,
            dst_ref=dst,
            send_sem=send_sem,
            recv_sem=recv_sem,
            device_id=device,
            device_id_type=MESH,
        )
        copy.start()
        return copy

    def peer(step):
        return lax.rem(me + step, nctx)

    def at_ctx(target):
        return (target, mine)

    def at_tp(target):
        return (me, target)

    def exchange(source, dest, send_sem, recv_sem):
        copies = []
        for step in range(1, nctx):
            target = peer(step)
            copies.append(
                send(
                    source.at[target],
                    dest.at[me],
                    send_sem.at[step],
                    recv_sem.at[step],
                    at_ctx(target),
                )
            )
        dest[me] = source[me]
        return copies

    def wait_all(copies):
        for copy in copies:
            copy.wait_recv()

    barrier = pltpu.get_barrier_semaphore()
    for step in range(1, nctx):
        pl.semaphore_signal(barrier, inc=1, device_id=at_ctx(peer(step)), device_id_type=MESH)
    for mate in (core_mate, side_mate):
        pl.semaphore_signal(barrier, inc=1, device_id=at_tp(mate), device_id_type=MESH)

    def pack_edges(picks, sources):
        total = None
        for index, source in enumerate(sources):
            block = merge_rows(source[...])
            term = lax.dot_general(
                picks[index], block, (((1,), (1,)), ((), ())), preferred_element_type=F32
            )
            total = term if total is None else total + term
        halo_out[...] = total.astype(BF16)

    def unpack_edges(picks):
        for index in range(3):
            spread = lax.dot_general(
                halo_in[...], picks[index], (((0,), (0,)), ((), ())), preferred_element_type=F32
            )
            edge[index] = spread.reshape(nctx, channels, width)

    loaded(0, 1, 2, 7)
    pack_edges(ends, (query, key, value))
    pl.semaphore_wait(barrier, nctx + 1)

    sent = []
    halo = send(halo_out, halo_in, halo_s.at[0], halo_r.at[0], at_ctx(peer(1)))
    loaded(6)
    own_rows = full_cot.at[pl.ds(mine * share, share)]
    to_side = send(cot, own_rows, cot_s.at[0], cot_r.at[0], at_tp(side_mate))
    to_core = send(cot, own_rows, cot_s.at[1], cot_r.at[1], at_tp(core_mate))
    sent += [to_side, to_core]
    full_cot[pl.ds(mine * share, share)] = cot[...]
    loaded(3)
    for index in range(3):
        padded = jnp.concatenate(
            [taps_in[index], jnp.zeros((taps.shape[3] - tap_count, nctx * channels), F32)], axis=0
        )
        taps[index] = padded.T.reshape(nctx, channels, taps.shape[3])

    table = make_tables(nctx, width)[0]

    def factor(part, k, n):
        if isinstance(k, int) and isinstance(n, int):
            return float(table[part, k, n])
        return outer[part, k, n]

    def spectrum(spec):
        def one(k, carry):
            re = im = None
            for n in range(nctx):
                block = signal[n]
                re = add_term(re, factor(0, k, n), block)
                im = add_term(im, factor(1, k, n), block)
            if im is None:
                im = jnp.zeros((channels, width), F32)
            cos, sin = twists[0, k], twists[1, k]
            rows = window(k, channels)
            work[rows, :width] = re * cos - im * sin
            work[rows, width:] = re * sin + im * cos
            return carry

        repeat(kept, one)
        spec[...] = dot_split(work[...], fwd_high[...], fwd_low[...])

    def inverse(re, im, store):
        work[:, :width] = re
        work[:, width:] = im
        work[...] = dot_split(work[...], bwd_high[...], bwd_low[...])

        def turn(k, carry):
            rows = window(k, channels)
            back_re, back_im = work[rows, :width], work[rows, width:]
            cos, sin = twists[2, k], twists[3, k]
            parts[0, k] = back_re * cos + back_im * sin
            parts[1, k] = back_im * cos - back_re * sin
            return carry

        repeat(kept, turn)

        def one(n, carry):
            total = parts[0, 0]
            for k in range(1, kept):
                total = add_term(total, factor(0, k, n), parts[0, k])
                if k < nctx:
                    total = add_term(total, factor(1, k, n), parts[1, k])
            store(n, total)
            return carry

        repeat(nctx, one)

    lane = lax.broadcasted_iota(jnp.int32, (channels, width), 1)

    loaded(4, 9, 10, 11)
    for n in range(nctx):
        signal[n] = filters[:, n * width : (n + 1) * width]
    spectrum(spec_f)

    halo.wait()
    unpack_edges(ends)
    has_before = me > 0

    def short(index):
        source = (query, key, value)[index]

        def one(m, carry):
            tap = taps[index, m]
            here = source[m].astype(F32)
            before = jnp.where(has_before, edge[index, m], 0.0)
            total = tap[:, 0:1] * here
            for j in range(1, tap_count):
                moved = pltpu.roll(jnp.where(lane >= width - j, before, here), j, 1)
                total = total + tap[:, j : j + 1] * moved
            shorts[index, m] = total.astype(BF16)
            return carry

        repeat(nctx, one)

    short(1)
    short(2)
    product[...] = (shorts[1].astype(F32) * shorts[2].astype(F32)).astype(BF16)
    product_copies = exchange(product, product_chan, product_s, product_r)
    sent += product_copies
    short(0)

    to_side.wait_recv()
    passed_rows = full_cot.at[pl.ds(side_mate * share, share)]
    passed = send(passed_rows, passed_rows, cot_s.at[2], cot_r.at[2], at_tp(core_mate))
    sent.append(passed)
    loaded(5, 8, 12, 13)
    to_core.wait_recv()

    def gate_part(group):
        cot_block = full_cot[pl.ds(group * share, share)].reshape(block_rows, width)
        start = pl.multiple_of(group * block_rows, block_rows)
        return lax.dot_general(
            cot_block,
            weight[pl.ds(start, block_rows), :],
            (((0,), (0,)), ((), ())),
            preferred_element_type=F32,
        )

    total = gate_part(mine) + gate_part(core_mate) + gate_part(side_mate)
    passed.wait_recv()
    total = total + gate_part(far_mate)
    grad_gated[...] = total.T.reshape(nctx, channels, width)
    grad_conv[...] = (grad_gated[...] * shorts[0].astype(F32)).astype(BF16)
    grad_copies = exchange(grad_conv, grad_conv_chan, grad_s, grad_r)
    sent += grad_copies

    wait_all(product_copies)
    signal[...] = product_chan[...].astype(F32)
    spectrum(spec_p)

    f_re, f_im = spec_f[:, :width], spec_f[:, width:]
    p_re, p_im = spec_p[:, :width], spec_p[:, width:]

    def store_convolved(n, total):
        conv_chan[n] = total.astype(BF16)

    inverse(p_re * f_re - p_im * f_im, p_re * f_im + p_im * f_re, store_convolved)
    conv_copies = exchange(conv_chan, conv_here, conv_s, conv_r)
    sent += conv_copies

    row_copies = []
    for step in range(1, nctx):
        target = peer(step)
        row_copies.append(
            send(
                full_cot.at[target, mine],
                cot_rows.at[mine, me],
                rows_s.at[step],
                rows_r.at[step],
                at_ctx(target),
            )
        )
    sent += row_copies
    cot_rows[mine, me] = full_cot[me, mine]

    wait_all(grad_copies)
    signal[...] = grad_conv_chan[...].astype(F32)
    spectrum(spec_g)
    f_re, f_im = spec_f[:, :width], spec_f[:, width:]
    g_re, g_im = spec_g[:, :width], spec_g[:, width:]

    def store_product(n, total):
        grad_chan[n] = total.astype(BF16)

    inverse(f_re * g_re + f_im * g_im, f_re * g_im - f_im * g_re, store_product)
    back_copies = exchange(grad_chan, grad_here, back_s, back_r)
    sent += back_copies

    wait_all(conv_copies)
    gated_all[me] = (shorts[0].astype(F32) * conv_here[...].astype(F32)).astype(BF16)
    line = nctx // 2
    place = me // 2

    def relay(step, way, action):
        sign = 1 - 2 * way
        block = gated_all.at[me - sign * 2 * step]
        return pltpu.make_async_remote_copy(
            src_ref=block,
            dst_ref=block,
            send_sem=all_s.at[way, step],
            recv_sem=all_r.at[way, step + 1 - action],
            device_id=at_ctx(me + sign * (2 - 4 * action)),
            device_id_type=MESH,
        )

    def came(step, way):
        return place >= step if way == 0 else place < line - step

    def goes(step, way):
        more = place < line - 1 if way == 0 else place > 0
        return more if step == 0 else jnp.logical_and(came(step, way), more)

    def to_mate(spot):
        block = gated_all.at[2 * spot + me % 2]
        return pltpu.make_async_remote_copy(
            src_ref=block,
            dst_ref=block,
            send_sem=fwd_s.at[spot],
            recv_sem=fwd_r.at[spot],
            device_id=at_ctx(x_mate),
            device_id_type=MESH,
        )

    def pass_on(step):
        for way in range(2):
            if step:

                @pl.when(came(step, way))
                def _():
                    relay(step, way, 1).wait_recv()

            if step < line - 1:

                @pl.when(goes(step, way))
                def _():
                    relay(step, way, 0).start()

            if step:

                @pl.when(came(step, way))
                def _():
                    to_mate(place - step * (1 - 2 * way)).start()

        if step == 0:
            to_mate(place).start()

    pass_on(0)

    right = merge_rows(gated_all[me])

    def project(group):
        start = pl.multiple_of(group * block_rows, block_rows)
        return dot(weight[pl.ds(start, block_rows), :], right)

    core = mine % 2
    pair_copies = []
    for side in range(ntp // 2):
        partial[side] = project(2 * side + 1 - core).astype(BF16)
        pair_copies.append(
            send(
                partial.at[side],
                pair_in.at[side],
                pair_s.at[side],
                pair_r.at[side],
                at_tp(core_mate),
            )
        )
    sent += pair_copies

    wait_all(row_copies)
    own_quarter = cot_rows.at[mine]
    quarter_side = send(own_quarter, own_quarter, quart_s.at[0], quart_r.at[0], at_tp(side_mate))
    quarter_core = send(own_quarter, own_quarter, quart_s.at[1], quart_r.at[1], at_tp(core_mate))
    sent += [quarter_side, quarter_core]

    wait_all(back_copies)

    def gradients(m, carry):
        back = grad_here[m].astype(F32)
        shorts_grad[0, m] = (grad_gated[m] * conv_here[m].astype(F32)).astype(BF16)
        shorts_grad[1, m] = (back * shorts[2, m].astype(F32)).astype(BF16)
        shorts_grad[2, m] = (back * shorts[1, m].astype(F32)).astype(BF16)
        return carry

    repeat(nctx, gradients)
    pack_edges(starts, [shorts_grad.at[index] for index in range(3)])
    halo = send(halo_out, halo_in, halo_s.at[1], halo_r.at[1], at_ctx(peer(nctx - 1)))

    my_side = mine // 2
    wait_all(pair_copies)
    pair_sum[...] = (project(side_mate) + pair_in[1 - my_side].astype(F32)).astype(BF16)
    final = send(pair_sum, final_in, final_s, final_r, at_tp(side_mate))
    sent.append(final)

    pass_on(1)

    halo.wait()
    unpack_edges(starts)
    has_after = me < nctx - 1
    for index, result in enumerate((grad_query, grad_key, grad_value)):

        def long(m, carry, index=index, result=result):
            tap = taps[index, m]
            here = shorts_grad[index, m].astype(F32)
            after = jnp.where(has_after, edge[index, m], 0.0)
            total = tap[:, 0:1] * here
            for j in range(1, tap_count):
                moved = pltpu.roll(jnp.where(lane < j, after, here), width - j, 1)
                total = total + tap[:, j : j + 1] * moved
            result[m] = total.astype(BF16)
            return carry

        repeat(nctx, long)
        store(1 + index)

    for step in range(2, line - 1):
        pass_on(step)

    p_re, p_im = spec_p[:, :width], spec_p[:, width:]
    g_re, g_im = spec_g[:, :width], spec_g[:, width:]

    def store_filters(n, total):
        grad_filters[:, window(n, width)] = total

    inverse(p_re * g_re + p_im * g_im, p_re * g_im - p_im * g_re, store_filters)
    store(4)
    if line > 2:
        pass_on(line - 1)
    quarter_side.wait_recv()
    far_quarter = cot_rows.at[side_mate]
    quarter_far = send(far_quarter, far_quarter, quart_s.at[2], quart_r.at[2], at_tp(core_mate))
    sent.append(quarter_far)

    own_sum = project(mine) + pair_in[my_side].astype(F32)
    final.wait_recv()
    mixed_out[...] = (own_sum + final_in[...].astype(F32)).astype(BF16)
    store(0)

    quarter_core.wait_recv()
    quarter_far.wait_recv()
    quarter = cot_rows.shape[2]

    def over_line(column):
        blocks = [merge_rows(gated_all[2 * spot + column]) for spot in range(line)]
        return jnp.concatenate(blocks, axis=1)

    def weigh(group, column, right):
        left = [cot_rows[group, 2 * spot + column] for spot in range(line)]
        return lax.dot_general(
            jnp.concatenate(left, axis=1),
            right,
            (((1,), (1,)), ((), ())),
            preferred_element_type=F32,
        )

    right = over_line(me % 2)
    for group in range(ntp):
        rows = slice(group * quarter, (group + 1) * quarter)
        grad_weight[rows, :] = weigh(group, me % 2, right)
    for spot in range(line):
        to_mate(spot).wait_recv()
    right = over_line(x_mate % 2)
    for group in range(ntp):
        rows = slice(group * quarter, (group + 1) * quarter)
        grad_weight[rows, :] += weigh(group, x_mate % 2, right)
        store(5, pl.ds(group * quarter, quarter), OUTPUTS - 1 + group)

    for copy in sent:
        copy.wait_send()
    for spot in range(line):
        to_mate(spot).wait_send()
    for step in range(line - 1):
        for way in range(2):

            @pl.when(goes(step, way))
            def _(step=step, way=way):
                relay(step, way, 0).wait_send()
    for copy in stores:
        copy.wait()


def hand_on(*refs):
    count = (len(refs) - 2) // 3
    sources, dests, held = refs[:count], refs[count : 2 * count], refs[2 * count : 3 * count]
    in_sem, out_sem = refs[3 * count :]
    loads = [
        pltpu.make_async_copy(source, place, in_sem.at[index])
        for index, (source, place) in enumerate(zip(sources, held))
    ]
    stores = [
        pltpu.make_async_copy(place, dest, out_sem.at[index])
        for index, (place, dest) in enumerate(zip(held, dests))
    ]
    for load in loads:
        load.start()
    for load, store in zip(loads, stores):
        load.wait()
        store.start()
    for store in stores:
        store.wait()


def per_device(nctx, ntp, query_in, key_in, value_in, short_weights, filters, out_weight, cotangent):
    rows, width = query_in.shape
    channels = rows // nctx
    features = out_weight.shape[0]
    quarter = features // (nctx * ntp)
    share = nctx // ntp
    kept = nctx + 1
    outer, twists, *inner = make_tables(nctx, width)
    tap_count = short_weights.shape[2]
    tap_slots = -(-tap_count // 8) * 8
    edge_rows = -(-3 * tap_slots // 16) * 16
    ends = np.zeros((3, edge_rows, width), np.float32)
    starts = np.zeros((3, edge_rows, width), np.float32)
    for index in range(3):
        for j in range(tap_count - 1):
            ends[index, index * tap_slots + j, width - (tap_count - 1) + j] = 1.0
            starts[index, index * tap_slots + j, j] = 1.0
    blocks = (nctx, channels, width)

    def bf(*shape):
        return pltpu.VMEM(shape, BF16)

    def f32(*shape):
        return pltpu.VMEM(shape, F32)

    def sems(*shape):
        return pltpu.SemaphoreType.DMA(shape)

    smem = pl.BlockSpec(memory_space=pltpu.SMEM)
    anywhere = pl.BlockSpec(memory_space=pl.ANY)
    out_shape = (
        jax.ShapeDtypeStruct((features // ntp, width), BF16),
        jax.ShapeDtypeStruct(blocks, BF16),
        jax.ShapeDtypeStruct(blocks, BF16),
        jax.ShapeDtypeStruct(blocks, BF16),
        jax.ShapeDtypeStruct((channels, nctx * width), F32),
        jax.ShapeDtypeStruct((features // nctx, rows), F32),
    )
    arrays = (
        query_in.reshape(blocks),
        key_in.reshape(blocks),
        value_in.reshape(blocks),
        short_weights.transpose(0, 2, 1),
        filters.reshape(channels, nctx * width),
        out_weight,
        cotangent.reshape(share, ntp, quarter, width),
        jnp.asarray(ends.astype(jnp.bfloat16)),
        jnp.asarray(starts.astype(jnp.bfloat16)),
        jnp.asarray(twists),
        *[jnp.asarray(table) for table in inner],
    )
    outs = pl.pallas_call(
        functools.partial(kernel, nctx, ntp),
        out_shape=out_shape,
        in_specs=[smem] + [anywhere] * INPUTS,
        out_specs=tuple([anywhere] * OUTPUTS),
        scratch_shapes=[pltpu.VMEM(array.shape, array.dtype) for array in arrays]
        + [pltpu.VMEM(shape.shape, shape.dtype) for shape in out_shape]
        + [
            sems(INPUTS),
            sems(OUTPUTS - 1 + ntp),
            bf(nctx, ntp, quarter, width),
            bf(ntp, nctx, quarter, width),
            f32(3, nctx, channels, tap_slots),
            bf(edge_rows, rows),
            bf(edge_rows, rows),
            f32(3, *blocks),
            bf(3, *blocks),
            f32(*blocks),
            f32(kept * channels, 2 * width),
            f32(2, kept, channels, width),
            f32(kept * channels, 2 * width),
            f32(kept * channels, 2 * width),
            f32(kept * channels, 2 * width),
            bf(*blocks),
            bf(*blocks),
            bf(*blocks),
            bf(*blocks),
            bf(nctx, *blocks),
            f32(*blocks),
            bf(*blocks),
            bf(*blocks),
            bf(*blocks),
            bf(*blocks),
            bf(3, *blocks),
            bf(ntp // 2, features // ntp, width),
            bf(ntp // 2, features // ntp, width),
            bf(features // ntp, width),
            bf(features // ntp, width),
            sems(2),
            sems(2),
            sems(3),
            sems(3),
            sems(nctx),
            sems(nctx),
            sems(3),
            sems(3),
            sems(nctx),
            sems(nctx),
            sems(nctx),
            sems(nctx),
            sems(nctx),
            sems(nctx),
            sems(nctx),
            sems(nctx),
            sems(2, nctx // 2),
            sems(2, nctx // 2),
            sems(nctx),
            sems(nctx),
            sems(ntp // 2),
            sems(ntp // 2),
            pltpu.SemaphoreType.DMA,
            pltpu.SemaphoreType.DMA,
        ],
        compiler_params=pltpu.CompilerParams(
            collective_id=0, has_side_effects=True, vmem_limit_bytes=56 * 1024 * 1024
        ),
        cost_estimate=pl.CostEstimate(
            flops=6 * features * rows * width, bytes_accessed=10 * features * rows // 4, transcendentals=0
        ),
        name="mixer",
    )(
        jnp.asarray(outer.astype(np.float32)),
        *arrays,
    )
    outs = pl.pallas_call(
        hand_on,
        out_shape=out_shape,
        in_specs=[anywhere] * OUTPUTS,
        out_specs=tuple([anywhere] * OUTPUTS),
        scratch_shapes=[pltpu.VMEM(shape.shape, shape.dtype) for shape in out_shape]
        + [sems(OUTPUTS), sems(OUTPUTS)],
        compiler_params=pltpu.CompilerParams(vmem_limit_bytes=56 * 1024 * 1024),
        name="hand_on",
    )(*outs)
    mixed, grad_query, grad_key, grad_value, grad_filters, grad_weight = outs
    return (
        mixed,
        grad_query.reshape(rows, width),
        grad_key.reshape(rows, width),
        grad_value.reshape(rows, width),
        grad_filters.reshape(filters.shape),
        grad_weight,
    )


def solution(mesh):
    placed = (
        P("tp", "ctx"),
        P("tp", "ctx"),
        P("tp", "ctx"),
        P(None, "tp", None),
        P("tp", "ctx", None),
        P(None, "tp"),
        P("tp", "ctx"),
    )
    return jax.shard_map(
        functools.partial(per_device, mesh.shape["ctx"], mesh.shape["tp"]),
        mesh=mesh,
        in_specs=placed,
        out_specs=(
            P("tp", "ctx"),
            P("tp", "ctx"),
            P("tp", "ctx"),
            P("tp", "ctx"),
            P("tp", "ctx", None),
            P("ctx", "tp"),
        ),
        check_vma=False,
    )
```
